512 devices in a mesh: kx: 64 (over z, x, core), gy: 8 (over y).
Axes of the slice: x: 4, y: 8, z: 8, core: 2. Of those that a mesh axis runs over, the one named last changes fastest.
Arguments:
- line_values: float32 [73728, 768], P(('kx', 'gy')), may hold values from -6 to 6
- line_ids: int32 [73728], P(('kx', 'gy')), may hold values from -1 to 147455, as said below
- line_start: int32 [73728], P(('kx', 'gy')), may hold values from 0 to 5, as said below
- line_stop: int32 [73728], P(('kx', 'gy')), may hold values from 1 to 6
- spectrum_real: float32 [64, 768, 768], P('kx', 'gy'), may hold values from -6 to 6
- spectrum_imag: float32 [64, 768, 768], P('kx', 'gy'), may hold values from -6 to 6
Outputs:
- product_real: float32 [64, 768, 768], P('kx', 'gy')
- product_imag: float32 [64, 768, 768], P('kx', 'gy')
The draws below stay inside these ranges and needn't reach their ends.
Inputs may be any that keep to these rules, and one draw needn't show every extreme that they name: `line_ids`: slot s belongs to device block s // 144, which is k * (number of gy devices) + g for the device at index k of kx and g of gy; a used slot there holds a line y * 384 + z with y in [g * 48, (g + 1) * 48) and z in [k * 6, (k + 1) * 6). No line is held twice. Each device block has at most 144 used slots, and some block has exactly 144. Every slot has line_start < line_stop.
All inputs are finite; a program needn't handle non-finite values.
Results may differ from the reference program's by a relative error of at most 0.0003.
Values sent between devices are 32-bit elements; how exact they have to be, the bound alone decides.
No kernel may reach another device: no remote copies, remote signals or barrier semaphores. Data moves between devices by JAX's collectives and lax.ppermute only.
A program may use at most 64 MiB of HBM per device.

```python
import math
import jax
import jax.numpy as jnp
from jax import lax

NG = 384
BLK = 64
NB = 6
KXW = 64
YD = 48
ZD = 6
LCAP = 144
LINES = 73728


def slot_lines(key):
    key = jax.random.fold_in(key, 11)
    device_count = LINES // LCAP
    per_device = YD * ZD
    gy_count = NG // YD
    key_first, key_second, key_busy, key_order = jax.random.split(key, 4)
    first_draw = jax.random.randint(key_first, (device_count,), 0, LCAP + 1)
    second_draw = jax.random.randint(key_second, (device_count,), 0, LCAP + 1)
    counts = LCAP // 4 + (LCAP - LCAP // 4) * first_draw // LCAP * second_draw // LCAP
    busiest = jax.random.randint(key_busy, (), 0, device_count)
    counts = jnp.where(jnp.arange(device_count) == busiest, LCAP, counts)
    orders = jax.vmap(lambda one_key: jax.random.permutation(one_key, per_device))(jax.random.split(key_order, device_count))
    chosen = orders[:, :LCAP]
    device = jnp.arange(device_count, dtype=jnp.int32)[:, None]
    kx_index = device // gy_count
    gy_index = device % gy_count
    row_value = gy_index * YD + chosen // ZD
    depth_value = kx_index * ZD + chosen % ZD
    slot_index = jnp.arange(LCAP, dtype=jnp.int32)[None, :]
    line_number = jnp.where(slot_index < counts[:, None], row_value * NG + depth_value, -1)
    return line_number.reshape(-1).astype(jnp.int32)


def chords(key):
    key = jax.random.fold_in(key, 12)
    key_start, key_extra = jax.random.split(key)
    start_block = jax.random.randint(key_start, (LINES,), 0, NB)
    extra_blocks = jax.random.randint(key_extra, (LINES,), 0, NB - start_block)
    stop_block = start_block + 1 + extra_blocks
    return (start_block.astype(jnp.int32), stop_block.astype(jnp.int32))


def draw_line_ids(key, part):
    key = jax.random.fold_in(key, 1)
    return slot_lines(key)


def draw_line_start(key, part):
    start_block, stop_block = chords(key)
    return start_block


def draw_line_stop(key, part):
    start_block, stop_block = chords(key)
    return stop_block


def block_levels(rng, shape, cuts, least, largest):
    loudness, own = 1.0, jax.random.fold_in(rng, 6)
    for dim, blocks in cuts:
        steps = jnp.exp(jax.random.uniform(jax.random.fold_in(own, dim), (blocks,), jnp.float32, least / len(cuts), largest / len(cuts)))
        loudness = loudness * jnp.repeat(steps, shape[dim] // blocks).reshape([-1 if axis == dim else 1 for axis in range(len(shape))])
    return loudness


def normal_values(rng, extent, spread, most, shards=(), kind=jnp.bfloat16):
    array = jax.random.normal(rng, extent, jnp.float32) * spread
    if len(shards) > 0:
        array = block_levels(rng, extent, shards, -0.22, 0.18) * array
    return jnp.clip(array, min=-most, max=most).astype(kind)


def setup_inputs(seed: int = 0) -> dict:
    streams_of = jax.random.split(jax.random.key(seed), 7)
    line_values = normal_values(streams_of[0], (LINES, 2 * NG), 1.0, 6.0, ((0, 512),), jnp.float32)
    line_ids = draw_line_ids(jax.random.fold_in(streams_of[6], 71), 0)
    line_start = draw_line_start(jax.random.fold_in(streams_of[6], 71), 0)
    line_stop = draw_line_stop(jax.random.fold_in(streams_of[6], 71), 0)
    spectrum_real = normal_values(streams_of[4], (KXW, 2 * NG, 2 * NG), 1.0, 6.0, ((0, 64), (1, 8)), jnp.float32)
    spectrum_imag = normal_values(streams_of[5], (KXW, 2 * NG, 2 * NG), 1.0, 6.0, ((0, 64), (1, 8)), jnp.float32)
    return {"line_values": line_values, "line_ids": line_ids, "line_start": line_start, "line_stop": line_stop, "spectrum_real": spectrum_real, "spectrum_imag": spectrum_imag}


HIGHEST = lax.Precision.HIGHEST


def angle_tables(inputs_count, outputs_count, length):
    rows_index = jnp.arange(inputs_count, dtype=jnp.int32)[:, None]
    wave_index = jnp.arange(outputs_count, dtype=jnp.int32)[None, :]
    phase_index = (rows_index * wave_index) % length
    angles = phase_index.astype(jnp.float32) * (2.0 * math.pi / length)
    return jnp.cos(angles), jnp.sin(angles)


def complex_table(inputs_count, outputs_count, length):
    cosine, sine_part = angle_tables(inputs_count, outputs_count, length)
    first_rows = jnp.concatenate([cosine, -sine_part], axis=1)
    second_rows = jnp.concatenate([sine_part, cosine], axis=1)
    return jnp.concatenate([first_rows, second_rows], axis=0)


def occupied_values(line_values, line_start, line_stop):
    position = jnp.arange(NG, dtype=jnp.int32)[None, :]
    inside = (position >= BLK * line_start[:, None]) & (position < BLK * line_stop[:, None])
    weight = inside.astype(jnp.float32)
    return line_values * jnp.concatenate([weight, weight], axis=1)


def reference(line_values, line_ids, line_start, line_stop, spectrum_real, spectrum_imag):
    values = occupied_values(line_values, line_start, line_stop)
    target = jnp.where(line_ids >= 0, line_ids, NG * NG).astype(jnp.int32)
    dense_grid = jnp.zeros((NG * NG, 2 * NG), jnp.float32).at[target].add(values, mode="drop")
    x_table = complex_table(NG, KXW, 2 * NG)
    x_spectrum = jnp.dot(dense_grid, x_table, precision=HIGHEST).reshape(NG, NG, 2, KXW)
    z_input = jnp.transpose(x_spectrum, (3, 0, 2, 1)).reshape(KXW * NG, 2 * NG)
    wave_table = complex_table(NG, 2 * NG, 2 * NG)
    z_spectrum = jnp.dot(z_input, wave_table, precision=HIGHEST).reshape(KXW, NG, 2, 2 * NG)
    y_input = jnp.transpose(z_spectrum, (0, 3, 2, 1)).reshape(KXW * 2 * NG, 2 * NG)
    full_spectrum = jnp.dot(y_input, wave_table, precision=HIGHEST).reshape(KXW, 2 * NG, 2, 2 * NG)
    real_part = full_spectrum[:, :, 0, :]
    imag_part = full_spectrum[:, :, 1, :]
    scale_factor = float(NG) ** -1.5
    product_real = scale_factor * (spectrum_real * real_part - spectrum_imag * imag_part)
    product_imag = scale_factor * (spectrum_real * imag_part + spectrum_imag * real_part)
    return product_real, product_imag
```

```python
import functools
import math

import jax
import jax.numpy as jnp
import ml_dtypes
import numpy as np
from jax import lax
from jax.experimental import pallas as pl
from jax.experimental.pallas import tpu as pltpu
from jax.sharding import PartitionSpec as P

NG = 384
BLK = 64
KXW = 64
YD = 48
ZD = 6
LCAP = 144
GY = 8
LINES_HERE = YD * ZD
WAVES = 128
F32 = jnp.float32
BF16 = jnp.bfloat16


def split(table):
    high = table.astype(np.float32).astype(ml_dtypes.bfloat16)
    low = (table - high.astype(np.float64)).astype(np.float32).astype(ml_dtypes.bfloat16)
    return high, low


def angles(first, second, length):
    return 2.0 * math.pi * ((first[:, None] * second[None, :]) % length) / length


def x_tables():
    angle = angles(np.arange(NG), np.arange(KXW), 2 * NG)
    c, s = np.cos(angle), np.sin(angle)
    return split(np.block([[c, -s], [s, c]]))


def wave_tables():
    angle = angles(np.arange(64), np.arange(WAVES), WAVES)
    c, s = np.cos(angle), np.sin(angle)
    high, low = split(np.block([[c, -s], [s, c]]))
    return np.concatenate([high, high, low], axis=0)


def twiddles():
    angle = angles(np.arange(6), np.arange(WAVES), 2 * NG)
    both = np.zeros((16, WAVES), np.float32)
    both[0:6] = np.cos(angle)
    both[8:14] = np.sin(angle)
    return both


def halves(values):
    high = values.astype(BF16)
    low = (values - high.astype(F32)).astype(BF16)
    return high, low


def dot(a, b):
    return jnp.dot(a, b, preferred_element_type=F32)


def dft3(v0, v1, v2):
    s3 = math.sqrt(3.0) / 2.0
    sum_re, sum_im = v1[0] + v2[0], v1[1] + v2[1]
    dif_re, dif_im = s3 * (v1[0] - v2[0]), s3 * (v1[1] - v2[1])
    mid_re, mid_im = v0[0] - 0.5 * sum_re, v0[1] - 0.5 * sum_im
    return (
        (v0[0] + sum_re, v0[1] + sum_im),
        (mid_re + dif_im, mid_im - dif_re),
        (mid_re - dif_im, mid_im + dif_re),
    )


def dft6(v):
    s3 = math.sqrt(3.0) / 2.0
    even = dft3(v[0], v[2], v[4])
    odd = dft3(v[1], v[3], v[5])
    turned = (
        odd[0],
        (0.5 * odd[1][0] + s3 * odd[1][1], 0.5 * odd[1][1] - s3 * odd[1][0]),
        (-0.5 * odd[2][0] + s3 * odd[2][1], -0.5 * odd[2][1] - s3 * odd[2][0]),
    )
    front = [(e[0] + o[0], e[1] + o[1]) for e, o in zip(even, turned)]
    back = [(e[0] - o[0], e[1] - o[1]) for e, o in zip(even, turned)]
    return front + back


def waves(rows, table_ref):
    high, low = halves(rows)
    both = jnp.concatenate([high, low], axis=1)
    return dot(both, table_ref[0:256]) + dot(high, table_ref[256:384])


def twisted(wave_rows, rows, twiddle_ref):
    terms = []
    for u in range(6):
        re = wave_rows[u * rows : (u + 1) * rows, 0:WAVES]
        im = wave_rows[u * rows : (u + 1) * rows, WAVES : 2 * WAVES]
        if u > 0:
            c, s = twiddle_ref[u : u + 1, :], twiddle_ref[8 + u : 9 + u, :]
            re, im = re * c + im * s, im * c - re * s
        terms.append((re, im))
    return dft6(terms)


def quotient(values, divisor):
    return jnp.floor((values + 0.5) * (1.0 / divisor))


def x_body(ids, start, stop, values, high_table, low_table):
    ids = ids.astype(F32)
    y = quotient(ids, NG)
    z = ids - NG * y
    z_here = z - ZD * quotient(z, ZD)
    y_here = y - YD * quotient(y, YD)
    t = quotient(y_here, 6)
    target = z_here * YD + (y_here - 6.0 * t) * 8.0 + t
    target = jnp.where(ids < 0, -1.0, target).astype(jnp.int32)
    bounds = jnp.concatenate(
        [start.astype(F32) * BLK, stop.astype(F32) * BLK, jnp.zeros((6, LCAP), F32)], axis=0
    )
    bounds = jnp.concatenate([bounds, jnp.zeros((8, 256 - LCAP), F32)], axis=1)
    columns = bounds.T[0:LCAP].astype(jnp.int32)
    position = lax.broadcasted_iota(jnp.int32, (LCAP, NG), 1)
    inside = (position >= columns[:, 0:1]) & (position < columns[:, 1:2])
    real = jnp.where(inside, values[:, 0:NG], 0.0)
    imag = jnp.where(inside, values[:, NG : 2 * NG], 0.0)
    high, low = halves(jnp.concatenate([real, imag], axis=1))
    spectrum = dot(high, high_table) + dot(low, high_table) + dot(high, low_table)
    place = lax.broadcasted_iota(jnp.int32, (LINES_HERE, LCAP), 0)
    chosen = jnp.where(place == target, 1.0, 0.0).astype(BF16)
    high, low = halves(spectrum)
    lines = dot(chosen, high) + dot(chosen, low)
    lines = jnp.concatenate(
        [
            lines[:, 0:KXW],
            lines[:, KXW : 2 * KXW],
            jnp.zeros((640 - 2 * LINES_HERE, KXW), F32),
        ],
        axis=0,
    )
    lines = jnp.concatenate([lines, jnp.zeros((640, KXW), F32)], axis=1)
    return lines.T[0:KXW, 0 : 2 * LINES_HERE]


def x_kernel(ids_ref, start_ref, stop_ref, values_ref, high_ref, low_ref, out_ref):
    out = x_body(
        ids_ref[...], start_ref[...], stop_ref[...], values_ref[...], high_ref[...], low_ref[...]
    )
    out_ref[:, 0, :] = out


def swap_blocks(tiles, roll):
    lane = lax.broadcasted_iota(jnp.int32, tiles[0].shape, 1)
    low64 = lane < 64
    even32 = (lane // 32) % 2 == 0
    q0, q1, q2, q3 = tiles
    q0, q2 = jnp.where(low64, q0, roll(q2, 64)), jnp.where(low64, roll(q0, 64), q2)
    q1, q3 = jnp.where(low64, q1, roll(q3, 64)), jnp.where(low64, roll(q1, 64), q3)
    q0, q1 = jnp.where(even32, q0, roll(q1, 32)), jnp.where(even32, roll(q0, 96), q1)
    q2, q3 = jnp.where(even32, q2, roll(q3, 32)), jnp.where(even32, roll(q2, 96), q3)
    return q0, q1, q2, q3


def lane_roll(values, shift):
    return pltpu.roll(values, shift, 1)


def z_body(arrived, table_ref, twiddle_ref, store, roll):
    rows = jnp.concatenate([arrived, jnp.zeros((KXW, 64), F32)], axis=1)
    rows = jnp.concatenate([rows, jnp.zeros((KXW, 640), F32)], axis=0).T
    real, imag = rows[0:LINES_HERE], rows[LINES_HERE : 2 * LINES_HERE]
    spectrum = waves(real + roll(imag, 64), table_ref)
    for j, (re, im) in enumerate(twisted(spectrum, YD, twiddle_ref)):
        tiles = swap_blocks((re[0:24], re[24:48], im[0:24], im[24:48]), roll)
        for a in range(4):
            piece = 4 * j + a
            store(piece // 3, piece % 3, tiles[a])


def z_kernel(in_ref, table_ref, twiddle_ref, out_ref):
    def store(block, third, tile):
        out_ref[block, third * 24 : third * 24 + 24, :] = tile

    z_body(in_ref[:, 0, :], table_ref, twiddle_ref, store, lane_roll)


def y_body(load, table_ref, twiddle_ref, roll):
    pieces = {}
    for third in range(3):
        for e in range(3):
            rows = jnp.concatenate(
                [load(g, third * 24 + e * 8) for g in range(GY)], axis=0
            )
            flipped = jnp.concatenate([rows, roll(rows, 64)], axis=0).T
            pieces[e, third] = flipped[0:32]
            pieces[3 + e, third] = flipped[32:64]
    rows = jnp.concatenate([pieces[u, third] for u in range(6) for third in range(3)], axis=0)
    return twisted(waves(rows, table_ref), 96, twiddle_ref)


def y_kernel(in_ref, real_ref, imag_ref, table_ref, twiddle_ref, out_re_ref, out_im_ref):
    scale = float(NG) ** (-1.5)

    def load(g, row):
        return in_ref[g, row : row + 8, :]

    for j, (re, im) in enumerate(y_body(load, table_ref, twiddle_ref, lane_roll)):
        lanes = slice(WAVES * j, WAVES * (j + 1))
        s_re, s_im = real_ref[0, :, lanes], imag_ref[0, :, lanes]
        re, im = scale * re, scale * im
        out_re_ref[0, :, lanes] = s_re * re - s_im * im
        out_im_ref[0, :, lanes] = s_re * im + s_im * re


PARAMS = pltpu.CompilerParams(vmem_limit_bytes=24 * 1024 * 1024)


def on_device(line_values, line_ids, line_start, line_stop, spectrum_real, spectrum_imag):
    high_x, low_x = x_tables()
    table = jnp.asarray(wave_tables())
    twiddle = jnp.asarray(twiddles())
    sent = pl.pallas_call(
        x_kernel,
        out_shape=jax.ShapeDtypeStruct((KXW, 1, 2 * LINES_HERE), F32),
        compiler_params=PARAMS,
        name="x_lines",
    )(
        line_ids.reshape(1, LCAP),
        line_start.reshape(1, LCAP),
        line_stop.reshape(1, LCAP),
        line_values,
        jnp.asarray(high_x),
        jnp.asarray(low_x),
    )
    arrived = lax.all_to_all(sent, "kx", split_axis=0, concat_axis=0, tiled=True)
    sent = pl.pallas_call(
        z_kernel,
        out_shape=jax.ShapeDtypeStruct((GY, 72, 128), F32),
        compiler_params=PARAMS,
        name="z_rows",
    )(arrived, table, twiddle)
    arrived = lax.all_to_all(sent, "gy", split_axis=0, concat_axis=0, tiled=True)
    out = jax.ShapeDtypeStruct(spectrum_real.shape, F32)
    return pl.pallas_call(
        y_kernel,
        out_shape=(out, out),
        compiler_params=PARAMS,
        name="y_rows",
    )(arrived, spectrum_real, spectrum_imag, table, twiddle)


def solution(mesh):
    in_specs = (
        P(("kx", "gy"), None),
        P(("kx", "gy")),
        P(("kx", "gy")),
        P(("kx", "gy")),
        P("kx", "gy", None),
        P("kx", "gy", None),
    )
    out_specs = (P("kx", "gy", None), P("kx", "gy", None))
    return jax.shard_map(
        on_device, mesh=mesh, in_specs=in_specs, out_specs=out_specs, check_vma=False
    )
```

```python
import functools
import math

import jax
import jax.numpy as jnp
import ml_dtypes
import numpy as np
from jax import lax
from jax.experimental import pallas as pl
from jax.experimental.pallas import tpu as pltpu
from jax.sharding import PartitionSpec as P

NG = 384
BLK = 64
KXW = 64
YD = 48
ZD = 6
LCAP = 144
GY = 8
LINES_HERE = YD * ZD
WAVES = 128
F32 = jnp.float32
BF16 = jnp.bfloat16


def split(table):
    high = table.astype(np.float32).astype(ml_dtypes.bfloat16)
    low = (table - high.astype(np.float64)).astype(np.float32).astype(ml_dtypes.bfloat16)
    return high, low


def angles(first, second, length):
    return 2.0 * math.pi * ((first[:, None] * second[None, :]) % length) / length


def x_tables():
    angle = angles(np.arange(NG), np.arange(KXW), 2 * NG)
    return np.concatenate([np.cos(angle), np.sin(angle)], axis=1).astype(np.float32)


def wave_tables():
    angle = angles(np.arange(64), np.arange(WAVES), WAVES)
    c, s = np.cos(angle), np.sin(angle)
    high, low = split(np.block([[c, -s], [s, c]]))
    return np.concatenate([high, high, low], axis=0)


def twiddles():
    angle = angles(np.arange(6), np.arange(WAVES), 2 * NG)
    both = np.zeros((16, WAVES), np.float32)
    both[0:6] = np.cos(angle)
    both[8:14] = np.sin(angle)
    return both


def halves(values):
    high = values.astype(BF16)
    low = (values - high.astype(F32)).astype(BF16)
    return high, low


def dot(a, b):
    return jnp.dot(a, b, preferred_element_type=F32)


def dft3(v0, v1, v2):
    s3 = math.sqrt(3.0) / 2.0
    sum_re, sum_im = v1[0] + v2[0], v1[1] + v2[1]
    dif_re, dif_im = s3 * (v1[0] - v2[0]), s3 * (v1[1] - v2[1])
    mid_re, mid_im = v0[0] - 0.5 * sum_re, v0[1] - 0.5 * sum_im
    return (
        (v0[0] + sum_re, v0[1] + sum_im),
        (mid_re + dif_im, mid_im - dif_re),
        (mid_re - dif_im, mid_im + dif_re),
    )


def dft6(v):
    s3 = math.sqrt(3.0) / 2.0
    even = dft3(v[0], v[2], v[4])
    odd = dft3(v[1], v[3], v[5])
    turned = (
        odd[0],
        (0.5 * odd[1][0] + s3 * odd[1][1], 0.5 * odd[1][1] - s3 * odd[1][0]),
        (-0.5 * odd[2][0] + s3 * odd[2][1], -0.5 * odd[2][1] - s3 * odd[2][0]),
    )
    front = [(e[0] + o[0], e[1] + o[1]) for e, o in zip(even, turned)]
    back = [(e[0] - o[0], e[1] - o[1]) for e, o in zip(even, turned)]
    return front + back


def waves(rows, table_ref):
    high, low = halves(rows)
    both = jnp.concatenate([high, low], axis=1)
    return dot(both, table_ref[0:256]) + dot(high, table_ref[256:384])


def twisted(wave_rows, rows, twiddle_ref):
    terms = []
    for u in range(6):
        re = wave_rows[u * rows : (u + 1) * rows, 0:WAVES]
        im = wave_rows[u * rows : (u + 1) * rows, WAVES : 2 * WAVES]
        if u > 0:
            c, s = twiddle_ref[u : u + 1, :], twiddle_ref[8 + u : 9 + u, :]
            re, im = re * c + im * s, im * c - re * s
        terms.append((re, im))
    return dft6(terms)


def quotient(values, divisor):
    return jnp.floor((values + 0.5) * (1.0 / divisor))


def columns_of(ids, start, stop):
    ids = ids.astype(F32)
    y = quotient(ids, NG)
    z = ids - NG * y
    z_here = z - ZD * quotient(z, ZD)
    y_here = y - YD * quotient(y, YD)
    t = quotient(y_here, 6)
    target = z_here * YD + (y_here - 6.0 * t) * 8.0 + t
    target = jnp.where(ids < 0, -1024.0, target)
    rows = [start.astype(F32) * BLK, stop.astype(F32) * BLK, target]
    rows = jnp.concatenate(rows + [jnp.zeros((5, LCAP), F32)], axis=0)
    rows = jnp.concatenate([rows, jnp.zeros((8, 256 - LCAP), F32)], axis=1)
    columns = rows.T[0:LCAP].astype(jnp.int32)
    return columns[:, 0:1], columns[:, 1:2], columns[:, 2:3]


def placements(target):
    place = lax.broadcasted_iota(jnp.int32, (LCAP, 640), 1)
    first = jnp.where(place == target, 1.0, 0.0).astype(BF16)
    second = jnp.where(place == target + LINES_HERE, 1.0, 0.0).astype(BF16)
    return first, second


def x_body(start, stop, first, second, values, table, roll):
    position = lax.broadcasted_iota(jnp.int32, (LCAP, NG), 1)
    inside = (position >= start) & (position < stop)
    real = jnp.where(inside, values[:, 0:NG], 0.0)
    imag = jnp.where(inside, values[:, NG : 2 * NG], 0.0)
    high, low = halves(jnp.concatenate([real, imag], axis=0))
    high_table, low_table = halves(table)
    sums = dot(high, high_table) + dot(low, high_table) + dot(high, low_table)
    lane = lax.broadcasted_iota(jnp.int32, (LCAP, 2 * KXW), 1)
    real = sums[0:LCAP]
    spectrum = jnp.where(lane < KXW, real, -real) + roll(sums[LCAP : 2 * LCAP], KXW)
    spectrum = jnp.concatenate([spectrum, jnp.zeros((256 - LCAP, 2 * KXW), F32)], axis=0)
    high, low = halves(spectrum.T[:, 0:LCAP])
    real = jnp.concatenate([high[0:KXW], low[0:KXW]], axis=0)
    imag = jnp.concatenate([high[KXW : 2 * KXW], low[KXW : 2 * KXW]], axis=0)
    placed = dot(real, first) + dot(imag, second)
    return (placed[0:KXW] + placed[KXW : 2 * KXW])[:, 0 : 2 * LINES_HERE]


def x_kernel(
    ids_hbm, start_hbm, stop_hbm, values_hbm, table_hbm, out_ref,
    ids_ref, start_ref, stop_ref, values_ref, table_ref, sems,
):
    pairs = [
        (ids_hbm, ids_ref),
        (start_hbm, start_ref),
        (stop_hbm, stop_ref),
        (values_hbm, values_ref),
        (table_hbm, table_ref),
    ]
    copies = [
        pltpu.make_async_copy(source, target, sems.at[i])
        for i, (source, target) in enumerate(pairs)
    ]
    for copy in copies:
        copy.start()
    for copy in copies[0:3]:
        copy.wait()
    start, stop, target = columns_of(ids_ref[...], start_ref[...], stop_ref[...])
    first, second = placements(target)
    copies[4].wait()
    copies[3].wait()
    out_ref[:, 0, :] = x_body(
        start, stop, first, second, values_ref[...], table_ref[...], lane_roll
    )


def swap_blocks(tiles, roll):
    lane = lax.broadcasted_iota(jnp.int32, tiles[0].shape, 1)
    low64 = lane < 64
    even32 = (lane // 32) % 2 == 0
    q0, q1, q2, q3 = tiles
    q0, q2 = jnp.where(low64, q0, roll(q2, 64)), jnp.where(low64, roll(q0, 64), q2)
    q1, q3 = jnp.where(low64, q1, roll(q3, 64)), jnp.where(low64, roll(q1, 64), q3)
    q0, q1 = jnp.where(even32, q0, roll(q1, 32)), jnp.where(even32, roll(q0, 96), q1)
    q2, q3 = jnp.where(even32, q2, roll(q3, 32)), jnp.where(even32, roll(q2, 96), q3)
    return q0, q1, q2, q3


def lane_roll(values, shift):
    return pltpu.roll(values, shift, 1)


def z_body(arrived, table_ref, twiddle_ref, store, roll):
    rows = jnp.concatenate([arrived, jnp.zeros((KXW, 64), F32)], axis=1)
    rows = jnp.concatenate([rows, jnp.zeros((KXW, 640), F32)], axis=0).T
    real, imag = rows[0:LINES_HERE], rows[LINES_HERE : 2 * LINES_HERE]
    spectrum = waves(real + roll(imag, 64), table_ref)
    for j, (re, im) in enumerate(twisted(spectrum, YD, twiddle_ref)):
        tiles = swap_blocks((re[0:24], re[24:48], im[0:24], im[24:48]), roll)
        for a in range(4):
            piece = 4 * j + a
            store(piece // 3, piece % 3, tiles[a])


def z_kernel(in_ref, table_ref, twiddle_ref, out_ref):
    def store(block, third, tile):
        out_ref[block, third * 24 : third * 24 + 24, :] = tile

    z_body(in_ref[:, 0, :], table_ref, twiddle_ref, store, lane_roll)


def y_third(load, third, table_ref, twiddle_ref, roll):
    pieces = {}
    for e in range(3):
        rows = jnp.concatenate([load(g, third * 24 + e * 8) for g in range(GY)], axis=0)
        flipped = jnp.concatenate([rows, roll(rows, 64)], axis=0).T
        pieces[e] = flipped[0:32]
        pieces[3 + e] = flipped[32:64]
    rows = jnp.concatenate([pieces[u] for u in range(6)], axis=0)
    return twisted(waves(rows, table_ref), 32, twiddle_ref)


def y_kernel(
    in_ref, real_ref, imag_ref, table_ref, twiddle_ref, out_re_hbm, out_im_hbm,
    out_re_ref, out_im_ref, sems,
):
    scale = float(NG) ** (-1.5)

    def load(g, row):
        return in_ref[g, row : row + 8, :]

    copies = []
    for third in range(3):
        rows = slice(32 * third, 32 * third + 32)
        for j, (re, im) in enumerate(y_third(load, third, table_ref, twiddle_ref, lane_roll)):
            lanes = slice(WAVES * j, WAVES * (j + 1))
            s_re, s_im = real_ref[0, rows, lanes], imag_ref[0, rows, lanes]
            re, im = scale * re, scale * im
            out_re_ref[0, rows, lanes] = s_re * re - s_im * im
            out_im_ref[0, rows, lanes] = s_re * im + s_im * re
        for i, (source, target) in enumerate(((out_re_ref, out_re_hbm), (out_im_ref, out_im_hbm))):
            copies.append(
                pltpu.make_async_copy(
                    source.at[:, rows, :], target.at[:, rows, :], sems.at[2 * third + i]
                )
            )
            copies[-1].start()
    for copy in copies:
        copy.wait()


PARAMS = pltpu.CompilerParams(vmem_limit_bytes=24 * 1024 * 1024)


def in_hbm(array):
    return pltpu.with_memory_space_constraint(array, pltpu.HBM)


def on_device(line_values, line_ids, line_start, line_stop, spectrum_real, spectrum_imag):
    table = jnp.asarray(wave_tables())
    twiddle = jnp.asarray(twiddles())
    hbm = pl.BlockSpec(memory_space=pltpu.HBM)
    vmem = pl.BlockSpec(memory_space=pltpu.VMEM)
    sent = pl.pallas_call(
        x_kernel,
        out_shape=jax.ShapeDtypeStruct((KXW, 1, 2 * LINES_HERE), F32),
        in_specs=[hbm] * 5,
        out_specs=vmem,
        scratch_shapes=[
            pltpu.VMEM((1, LCAP), jnp.int32),
            pltpu.VMEM((1, LCAP), jnp.int32),
            pltpu.VMEM((1, LCAP), jnp.int32),
            pltpu.VMEM((LCAP, 2 * NG), F32),
            pltpu.VMEM((NG, 2 * KXW), F32),
            pltpu.SemaphoreType.DMA((5,)),
        ],
        compiler_params=PARAMS,
        name="x_lines",
    )(
        in_hbm(line_ids.reshape(1, LCAP)),
        in_hbm(line_start.reshape(1, LCAP)),
        in_hbm(line_stop.reshape(1, LCAP)),
        in_hbm(line_values),
        in_hbm(jnp.asarray(x_tables())),
    )
    arrived = lax.all_to_all(sent, "kx", split_axis=0, concat_axis=0, tiled=True)
    sent = pl.pallas_call(
        z_kernel,
        out_shape=jax.ShapeDtypeStruct((GY, 72, 128), F32),
        compiler_params=PARAMS,
        name="z_rows",
    )(arrived, table, twiddle)
    arrived = lax.all_to_all(sent, "gy", split_axis=0, concat_axis=0, tiled=True)
    out = jax.ShapeDtypeStruct(spectrum_real.shape, F32)
    return pl.pallas_call(
        y_kernel,
        out_shape=(out, out),
        in_specs=[vmem] * 5,
        out_specs=(hbm, hbm),
        scratch_shapes=[
            pltpu.VMEM(spectrum_real.shape, F32),
            pltpu.VMEM(spectrum_real.shape, F32),
            pltpu.SemaphoreType.DMA((6,)),
        ],
        compiler_params=PARAMS,
        name="y_rows",
    )(arrived, spectrum_real, spectrum_imag, table, twiddle)


def solution(mesh):
    in_specs = (
        P(("kx", "gy"), None),
        P(("kx", "gy")),
        P(("kx", "gy")),
        P(("kx", "gy")),
        P("kx", "gy", None),
        P("kx", "gy", None),
    )
    out_specs = (P("kx", "gy", None), P("kx", "gy", None))
    return jax.shard_map(
        on_device, mesh=mesh, in_specs=in_specs, out_specs=out_specs, check_vma=False
    )
```

```python
import functools
import math

import jax
import jax.numpy as jnp
import ml_dtypes
import numpy as np
from jax import lax
from jax.experimental import pallas as pl
from jax.experimental.pallas import tpu as pltpu
from jax.sharding import PartitionSpec as P

NG = 384
BLK = 64
KXW = 64
YD = 48
ZD = 6
LCAP = 144
GY = 8
LINES_HERE = YD * ZD
WAVES = 128
F32 = jnp.float32
BF16 = jnp.bfloat16


KX_FIRST = (6, 2, 1)
GY_FIRST = 4


def kx_order():
    z_first, x_first, core_first = KX_FIRST
    return [
        ((z + z_first) % 8) * 8 + ((x + x_first) % 4) * 2 + (core + core_first) % 2
        for z in range(8)
        for x in range(4)
        for core in range(2)
    ]


def gy_order():
    return [(y + GY_FIRST) % GY for y in range(GY)]


def split(table):
    high = table.astype(np.float32).astype(ml_dtypes.bfloat16)
    low = (table - high.astype(np.float64)).astype(np.float32).astype(ml_dtypes.bfloat16)
    return high, low


def angles(first, second, length):
    return 2.0 * math.pi * ((first[:, None] * second[None, :]) % length) / length


def x_tables():
    angle = angles(np.arange(NG), np.array(kx_order()), 2 * NG)
    return np.concatenate([np.cos(angle), np.sin(angle)], axis=1).astype(np.float32)


def wave_tables(order):
    angle = angles(np.array(order), np.arange(WAVES), WAVES)
    c, s = np.cos(angle), np.sin(angle)
    high, low = split(np.block([[c, -s], [s, c]]))
    return np.concatenate([high, high, low], axis=0)


def twiddles():
    angle = angles(np.arange(6), np.arange(WAVES), 2 * NG)
    both = np.zeros((16, WAVES), np.float32)
    both[0:6] = np.cos(angle)
    both[8:14] = np.sin(angle)
    return both


def halves(values):
    high = values.astype(BF16)
    low = (values - high.astype(F32)).astype(BF16)
    return high, low


def dot(a, b):
    return jnp.dot(a, b, preferred_element_type=F32)


def dft3(v0, v1, v2):
    s3 = math.sqrt(3.0) / 2.0
    sum_re, sum_im = v1[0] + v2[0], v1[1] + v2[1]
    dif_re, dif_im = s3 * (v1[0] - v2[0]), s3 * (v1[1] - v2[1])
    mid_re, mid_im = v0[0] - 0.5 * sum_re, v0[1] - 0.5 * sum_im
    return (
        (v0[0] + sum_re, v0[1] + sum_im),
        (mid_re + dif_im, mid_im - dif_re),
        (mid_re - dif_im, mid_im + dif_re),
    )


def dft6(v):
    s3 = math.sqrt(3.0) / 2.0
    even = dft3(v[0], v[2], v[4])
    odd = dft3(v[1], v[3], v[5])
    turned = (
        odd[0],
        (0.5 * odd[1][0] + s3 * odd[1][1], 0.5 * odd[1][1] - s3 * odd[1][0]),
        (-0.5 * odd[2][0] + s3 * odd[2][1], -0.5 * odd[2][1] - s3 * odd[2][0]),
    )
    front = [(e[0] + o[0], e[1] + o[1]) for e, o in zip(even, turned)]
    back = [(e[0] - o[0], e[1] - o[1]) for e, o in zip(even, turned)]
    return front + back


def waves(rows, table_ref):
    high, low = halves(rows)
    both = jnp.concatenate([high, low], axis=1)
    return dot(both, table_ref[0:256]) + dot(high, table_ref[256:384])


def twisted(wave_rows, rows, twiddle_ref):
    terms = []
    for u in range(6):
        re = wave_rows[u * rows : (u + 1) * rows, 0:WAVES]
        im = wave_rows[u * rows : (u + 1) * rows, WAVES : 2 * WAVES]
        if u > 0:
            c, s = twiddle_ref[u : u + 1, :], twiddle_ref[8 + u : 9 + u, :]
            re, im = re * c + im * s, im * c - re * s
        terms.append((re, im))
    return dft6(terms)


def quotient(values, divisor):
    return jnp.floor((values + 0.5) * (1.0 / divisor))


def columns_of(ids, start, stop):
    ids = ids.astype(F32)
    y = quotient(ids, NG)
    z = ids - NG * y
    z_here = z - ZD * quotient(z, ZD)
    y_here = y - YD * quotient(y, YD)
    t = quotient(y_here, 6)
    target = z_here * YD + (y_here - 6.0 * t) * 8.0 + t
    target = jnp.where(ids < 0, -1024.0, target)
    rows = [start.astype(F32) * BLK, stop.astype(F32) * BLK, target]
    rows = jnp.concatenate(rows + [jnp.zeros((5, LCAP), F32)], axis=0)
    rows = jnp.concatenate([rows, jnp.zeros((8, 256 - LCAP), F32)], axis=1)
    columns = rows.T[0:LCAP].astype(jnp.int32)
    return columns[:, 0:1], columns[:, 1:2], columns[:, 2:3]


def placements(target):
    place = lax.broadcasted_iota(jnp.int32, (LCAP, 640), 1)
    first = jnp.where(place == target, 1.0, 0.0).astype(BF16)
    second = jnp.where(place == target + LINES_HERE, 1.0, 0.0).astype(BF16)
    return first, second


def x_body(start, stop, first, second, values, table, roll):
    position = lax.broadcasted_iota(jnp.int32, (LCAP, NG), 1)
    inside = (position >= start) & (position < stop)
    real = jnp.where(inside, values[:, 0:NG], 0.0)
    imag = jnp.where(inside, values[:, NG : 2 * NG], 0.0)
    high, low = halves(jnp.concatenate([real, imag], axis=0))
    high_table, low_table = halves(table)
    sums = dot(high, high_table) + dot(low, high_table) + dot(high, low_table)
    lane = lax.broadcasted_iota(jnp.int32, (LCAP, 2 * KXW), 1)
    real = sums[0:LCAP]
    spectrum = jnp.where(lane < KXW, real, -real) + roll(sums[LCAP : 2 * LCAP], KXW)
    spectrum = jnp.concatenate([spectrum, jnp.zeros((256 - LCAP, 2 * KXW), F32)], axis=0)
    high, low = halves(spectrum.T[:, 0:LCAP])
    real = jnp.concatenate([high[0:KXW], low[0:KXW]], axis=0)
    imag = jnp.concatenate([high[KXW : 2 * KXW], low[KXW : 2 * KXW]], axis=0)
    placed = dot(real, first) + dot(imag, second)
    return (placed[0:KXW] + placed[KXW : 2 * KXW])[:, 0 : 2 * LINES_HERE]


def x_kernel(
    ids_hbm, start_hbm, stop_hbm, values_hbm, table_hbm, out_ref,
    ids_ref, start_ref, stop_ref, values_ref, table_ref, sems,
):
    pairs = [
        (ids_hbm, ids_ref),
        (start_hbm, start_ref),
        (stop_hbm, stop_ref),
        (values_hbm, values_ref),
        (table_hbm, table_ref),
    ]
    copies = [
        pltpu.make_async_copy(source, target, sems.at[i])
        for i, (source, target) in enumerate(pairs)
    ]
    for copy in copies:
        copy.start()
    for copy in copies[0:3]:
        copy.wait()
    start, stop, target = columns_of(ids_ref[...], start_ref[...], stop_ref[...])
    first, second = placements(target)
    copies[4].wait()
    copies[3].wait()
    out_ref[:, 0, :] = x_body(
        start, stop, first, second, values_ref[...], table_ref[...], lane_roll
    )


def swap_blocks(tiles, roll):
    lane = lax.broadcasted_iota(jnp.int32, tiles[0].shape, 1)
    low64 = lane < 64
    even32 = (lane // 32) % 2 == 0
    q0, q1, q2, q3 = tiles
    q0, q2 = jnp.where(low64, q0, roll(q2, 64)), jnp.where(low64, roll(q0, 64), q2)
    q1, q3 = jnp.where(low64, q1, roll(q3, 64)), jnp.where(low64, roll(q1, 64), q3)
    q0, q1 = jnp.where(even32, q0, roll(q1, 32)), jnp.where(even32, roll(q0, 96), q1)
    q2, q3 = jnp.where(even32, q2, roll(q3, 32)), jnp.where(even32, roll(q2, 96), q3)
    return q0, q1, q2, q3


def lane_roll(values, shift):
    return pltpu.roll(values, shift, 1)


def z_body(arrived, table_ref, twiddle_ref, store, roll):
    rows = jnp.concatenate([arrived, jnp.zeros((KXW, 64), F32)], axis=1)
    rows = jnp.concatenate([rows, jnp.zeros((KXW, 640), F32)], axis=0).T
    real, imag = rows[0:LINES_HERE], rows[LINES_HERE : 2 * LINES_HERE]
    spectrum = waves(real + roll(imag, 64), table_ref)
    for j, (re, im) in enumerate(twisted(spectrum, YD, twiddle_ref)):
        tiles = swap_blocks((re[0:24], re[24:48], im[0:24], im[24:48]), roll)
        for a in range(4):
            piece = 4 * j + a
            store((piece // 3 - GY_FIRST) % GY, piece % 3, tiles[a])


def z_kernel(in_ref, table_ref, twiddle_ref, out_ref):
    def store(block, third, tile):
        out_ref[block, third * 24 : third * 24 + 24, :] = tile

    z_body(in_ref[:, 0, :], table_ref, twiddle_ref, store, lane_roll)


def y_third(load, third, table_ref, twiddle_ref, roll):
    pieces = {}
    for e in range(3):
        rows = jnp.concatenate([load((g - GY_FIRST) % GY, third * 24 + e * 8) for g in range(GY)], axis=0)
        flipped = jnp.concatenate([rows, roll(rows, 64)], axis=0).T
        pieces[e] = flipped[0:32]
        pieces[3 + e] = flipped[32:64]
    rows = jnp.concatenate([pieces[u] for u in range(6)], axis=0)
    return twisted(waves(rows, table_ref), 32, twiddle_ref)


def y_kernel(
    in_ref, real_ref, imag_ref, table_ref, twiddle_ref, out_re_hbm, out_im_hbm,
    out_re_ref, out_im_ref, sems,
):
    scale = float(NG) ** (-1.5)

    def load(g, row):
        return in_ref[g, row : row + 8, :]

    copies = []
    for third in range(3):
        rows = slice(32 * third, 32 * third + 32)
        for j, (re, im) in enumerate(y_third(load, third, table_ref, twiddle_ref, lane_roll)):
            lanes = slice(WAVES * j, WAVES * (j + 1))
            s_re, s_im = real_ref[0, rows, lanes], imag_ref[0, rows, lanes]
            re, im = scale * re, scale * im
            out_re_ref[0, rows, lanes] = s_re * re - s_im * im
            out_im_ref[0, rows, lanes] = s_re * im + s_im * re
        for i, (source, target) in enumerate(((out_re_ref, out_re_hbm), (out_im_ref, out_im_hbm))):
            copies.append(
                pltpu.make_async_copy(
                    source.at[:, rows, :], target.at[:, rows, :], sems.at[2 * third + i]
                )
            )
            copies[-1].start()
    for copy in copies:
        copy.wait()


PARAMS = pltpu.CompilerParams(vmem_limit_bytes=24 * 1024 * 1024)


def exchange(sent, axis, order):
    return lax.all_to_all(
        sent, axis, split_axis=0, concat_axis=0, tiled=True, axis_index_groups=[order]
    )


def in_hbm(array):
    return pltpu.with_memory_space_constraint(array, pltpu.HBM)


def on_device(line_values, line_ids, line_start, line_stop, spectrum_real, spectrum_imag):
    z_table = jnp.asarray(wave_tables(kx_order()))
    y_table = jnp.asarray(wave_tables(range(64)))
    twiddle = jnp.asarray(twiddles())
    hbm = pl.BlockSpec(memory_space=pltpu.HBM)
    vmem = pl.BlockSpec(memory_space=pltpu.VMEM)
    sent = pl.pallas_call(
        x_kernel,
        out_shape=jax.ShapeDtypeStruct((KXW, 1, 2 * LINES_HERE), F32),
        in_specs=[hbm] * 5,
        out_specs=vmem,
        scratch_shapes=[
            pltpu.VMEM((1, LCAP), jnp.int32),
            pltpu.VMEM((1, LCAP), jnp.int32),
            pltpu.VMEM((1, LCAP), jnp.int32),
            pltpu.VMEM((LCAP, 2 * NG), F32),
            pltpu.VMEM((NG, 2 * KXW), F32),
            pltpu.SemaphoreType.DMA((5,)),
        ],
        compiler_params=PARAMS,
        name="x_lines",
    )(
        in_hbm(line_ids.reshape(1, LCAP)),
        in_hbm(line_start.reshape(1, LCAP)),
        in_hbm(line_stop.reshape(1, LCAP)),
        in_hbm(line_values),
        in_hbm(jnp.asarray(x_tables())),
    )
    arrived = exchange(sent, "kx", kx_order())
    sent = pl.pallas_call(
        z_kernel,
        out_shape=jax.ShapeDtypeStruct((GY, 72, 128), F32),
        compiler_params=PARAMS,
        name="z_rows",
    )(arrived, z_table, twiddle)
    arrived = exchange(sent, "gy", gy_order())
    out = jax.ShapeDtypeStruct(spectrum_real.shape, F32)
    return pl.pallas_call(
        y_kernel,
        out_shape=(out, out),
        in_specs=[vmem] * 5,
        out_specs=(hbm, hbm),
        scratch_shapes=[
            pltpu.VMEM(spectrum_real.shape, F32),
            pltpu.VMEM(spectrum_real.shape, F32),
            pltpu.SemaphoreType.DMA((6,)),
        ],
        compiler_params=PARAMS,
        name="y_rows",
    )(arrived, spectrum_real, spectrum_imag, y_table, twiddle)


def solution(mesh):
    in_specs = (
        P(("kx", "gy"), None),
        P(("kx", "gy")),
        P(("kx", "gy")),
        P(("kx", "gy")),
        P("kx", "gy", None),
        P("kx", "gy", None),
    )
    out_specs = (P("kx", "gy", None), P("kx", "gy", None))
    return jax.shard_map(
        on_device, mesh=mesh, in_specs=in_specs, out_specs=out_specs, check_vma=False
    )
```

```python
import functools
import math

import jax
import jax.numpy as jnp
import ml_dtypes
import numpy as np
from jax import lax
from jax.experimental import pallas as pl
from jax.experimental.pallas import tpu as pltpu
from jax.sharding import PartitionSpec as P

NG = 384
BLK = 64
KXW = 64
YD = 48
ZD = 6
LCAP = 144
GY = 8
LINES_HERE = YD * ZD
WAVES = 128
F32 = jnp.float32
BF16 = jnp.bfloat16


KX_ORDER = [
    ((z + 7) % 8) * 8 + ((x + 2) % 4) * 2 + 1 - core
    for z in range(8)
    for x in range(4)
    for core in range(2)
]
GY_ORDER = [(y + 5) % GY for y in range(GY)]


def split(table):
    high = table.astype(np.float32).astype(ml_dtypes.bfloat16)
    low = (table - high.astype(np.float64)).astype(np.float32).astype(ml_dtypes.bfloat16)
    return high, low


def angles(first, second, length):
    return 2.0 * math.pi * ((first[:, None] * second[None, :]) % length) / length


def x_tables():
    angle = angles(np.arange(NG), np.array(KX_ORDER), 2 * NG)
    return np.concatenate(split(np.concatenate([np.cos(angle), np.sin(angle)], axis=1)), axis=1)


def wave_tables(order):
    angle = angles(np.array(order), np.arange(WAVES), WAVES)
    c, s = np.cos(angle), np.sin(angle)
    high, low = split(np.block([[c, -s], [s, c]]))
    return np.concatenate([high, high, low], axis=0)


def twiddles():
    angle = angles(np.arange(6), np.arange(WAVES), 2 * NG)
    both = np.zeros((16, WAVES), np.float32)
    both[0:6] = np.cos(angle)
    both[8:14] = np.sin(angle)
    return both


def halves(values):
    high = values.astype(BF16)
    low = (values - high.astype(F32)).astype(BF16)
    return high, low


def dot(a, b):
    return jnp.dot(a, b, preferred_element_type=F32)


def dft3(v0, v1, v2):
    s3 = math.sqrt(3.0) / 2.0
    sum_re, sum_im = v1[0] + v2[0], v1[1] + v2[1]
    dif_re, dif_im = s3 * (v1[0] - v2[0]), s3 * (v1[1] - v2[1])
    mid_re, mid_im = v0[0] - 0.5 * sum_re, v0[1] - 0.5 * sum_im
    return (
        (v0[0] + sum_re, v0[1] + sum_im),
        (mid_re + dif_im, mid_im - dif_re),
        (mid_re - dif_im, mid_im + dif_re),
    )


def dft6(v):
    s3 = math.sqrt(3.0) / 2.0
    even = dft3(v[0], v[2], v[4])
    odd = dft3(v[1], v[3], v[5])
    turned = (
        odd[0],
        (0.5 * odd[1][0] + s3 * odd[1][1], 0.5 * odd[1][1] - s3 * odd[1][0]),
        (-0.5 * odd[2][0] + s3 * odd[2][1], -0.5 * odd[2][1] - s3 * odd[2][0]),
    )
    front = [(e[0] + o[0], e[1] + o[1]) for e, o in zip(even, turned)]
    back = [(e[0] - o[0], e[1] - o[1]) for e, o in zip(even, turned)]
    return front + back


def waves(rows, table_ref):
    high, low = halves(rows)
    both = jnp.concatenate([high, low], axis=1)
    return dot(both, table_ref[0:256]) + dot(high, table_ref[256:384])


def twisted(wave_rows, rows, twiddle_ref):
    terms = []
    for u in range(6):
        re = wave_rows[u * rows : (u + 1) * rows, 0:WAVES]
        im = wave_rows[u * rows : (u + 1) * rows, WAVES : 2 * WAVES]
        if u > 0:
            c, s = twiddle_ref[u : u + 1, :], twiddle_ref[8 + u : 9 + u, :]
            re, im = re * c + im * s, im * c - re * s
        terms.append((re, im))
    return dft6(terms)


def quotient(values, divisor):
    return jnp.floor((values + 0.5) * (1.0 / divisor))


def lines_of(ids):
    ids = ids.astype(F32)
    y = quotient(ids, NG)
    z = ids - NG * y
    z_here = z - ZD * quotient(z, ZD)
    y_here = y - YD * quotient(y, YD)
    t = quotient(y_here, 6)
    target = z_here * YD + (y_here - 6.0 * t) * 8.0 + t
    target = jnp.where(ids < 0, -1.0, target).astype(jnp.int32)
    place = lax.broadcasted_iota(jnp.int32, (LINES_HERE, LCAP), 0)
    return jnp.where(place == target, 1.0, 0.0).astype(BF16)


def cells_of(start, stop):
    rows = [start.astype(F32) * BLK, stop.astype(F32) * BLK, jnp.zeros((6, LCAP), F32)]
    rows = jnp.concatenate(rows, axis=0)
    rows = jnp.concatenate([rows, jnp.zeros((8, 256 - LCAP), F32)], axis=1)
    columns = rows.T[0:LCAP].astype(jnp.int32)
    return columns[:, 0:1], columns[:, 1:2]


def x_body(start, stop, chosen, values, table, roll):
    position = lax.broadcasted_iota(jnp.int32, (LCAP, NG), 1)
    inside = (position >= start) & (position < stop)
    real = jnp.where(inside, values[:, 0:NG], 0.0)
    imag = jnp.where(inside, values[:, NG : 2 * NG], 0.0)
    high, low = halves(jnp.concatenate([real, imag], axis=0))
    sums = dot(jnp.concatenate([high, low], axis=0), table)
    sums = sums[:, 0 : 2 * KXW] + sums[:, 2 * KXW : 4 * KXW]
    sums = sums[0 : 2 * LCAP] + sums[2 * LCAP : 4 * LCAP]
    lane = lax.broadcasted_iota(jnp.int32, (LCAP, 2 * KXW), 1)
    real = sums[0:LCAP]
    spectrum = jnp.where(lane < KXW, real, -real) + roll(sums[LCAP : 2 * LCAP], KXW)
    placed = dot(chosen, jnp.concatenate(halves(spectrum), axis=1))
    placed = placed[:, 0 : 2 * KXW] + placed[:, 2 * KXW : 4 * KXW]
    placed = jnp.concatenate([placed, jnp.zeros((384 - LINES_HERE, 2 * KXW), F32)], axis=0).T
    real, imag = placed[0:KXW], roll(placed[KXW : 2 * KXW], LINES_HERE - 256)
    lane = lax.broadcasted_iota(jnp.int32, (KXW, 128), 1)
    middle = jnp.where(lane < LINES_HERE - 256, real[:, 256:384], imag[:, 0:128])
    words = [real[:, 0:256], middle, imag[:, 128 : 2 * LINES_HERE - 256]]
    return jnp.concatenate(words, axis=1)


def x_kernel(
    ids_hbm, start_hbm, stop_hbm, values_hbm, table_hbm, out_ref,
    ids_ref, start_ref, stop_ref, values_ref, table_ref, sems,
):
    pairs = [
        (ids_hbm, ids_ref),
        (start_hbm, start_ref),
        (stop_hbm, stop_ref),
        (values_hbm, values_ref),
        (table_hbm, table_ref),
    ]
    copies = [
        pltpu.make_async_copy(source, target, sems.at[i])
        for i, (source, target) in enumerate(pairs)
    ]
    for copy in copies:
        copy.start()
    for copy in copies[0:3]:
        copy.wait()
    chosen = lines_of(ids_ref[...])
    start, stop = cells_of(start_ref[...], stop_ref[...])
    copies[4].wait()
    copies[3].wait()
    out_ref[:, 0, :] = x_body(
        start, stop, chosen, values_ref[...], table_ref[...], lane_roll
    )


def swap_blocks(tiles, roll):
    lane = lax.broadcasted_iota(jnp.int32, tiles[0].shape, 1)
    low64 = lane < 64
    even32 = (lane // 32) % 2 == 0
    q0, q1, q2, q3 = tiles
    q0, q2 = jnp.where(low64, q0, roll(q2, 64)), jnp.where(low64, roll(q0, 64), q2)
    q1, q3 = jnp.where(low64, q1, roll(q3, 64)), jnp.where(low64, roll(q1, 64), q3)
    q0, q1 = jnp.where(even32, q0, roll(q1, 32)), jnp.where(even32, roll(q0, 96), q1)
    q2, q3 = jnp.where(even32, q2, roll(q3, 32)), jnp.where(even32, roll(q2, 96), q3)
    return q0, q1, q2, q3


def lane_roll(values, shift):
    return pltpu.roll(values, shift, 1)


def z_body(arrived, table_ref, twiddle_ref, store, roll):
    rows = jnp.concatenate([arrived, jnp.zeros((KXW, 64), F32)], axis=1)
    rows = jnp.concatenate([rows, jnp.zeros((KXW, 640), F32)], axis=0).T
    real, imag = rows[0:LINES_HERE], rows[LINES_HERE : 2 * LINES_HERE]
    spectrum = waves(real + roll(imag, 64), table_ref)
    for j, (re, im) in enumerate(twisted(spectrum, YD, twiddle_ref)):
        tiles = swap_blocks((re[0:24], re[24:48], im[0:24], im[24:48]), roll)
        for a in range(4):
            piece = 4 * j + a
            store(GY_ORDER.index(piece // 3), piece % 3, tiles[a])


def z_kernel(in_ref, table_ref, twiddle_ref, out_ref):
    def store(block, third, tile):
        out_ref[block, third * 24 : third * 24 + 24, :] = tile

    z_body(in_ref[:, 0, :], table_ref, twiddle_ref, store, lane_roll)


def y_third(load, third, table_ref, twiddle_ref, roll):
    pieces = {}
    for e in range(3):
        rows = jnp.concatenate([load(GY_ORDER.index(g), third * 24 + e * 8) for g in range(GY)], axis=0)
        flipped = jnp.concatenate([rows, roll(rows, 64)], axis=0).T
        pieces[e] = flipped[0:32]
        pieces[3 + e] = flipped[32:64]
    rows = jnp.concatenate([pieces[u] for u in range(6)], axis=0)
    return twisted(waves(rows, table_ref), 32, twiddle_ref)


def y_kernel(
    in_ref, real_ref, imag_ref, table_ref, twiddle_ref, out_re_hbm, out_im_hbm,
    out_re_ref, out_im_ref, sems,
):
    scale = float(NG) ** (-1.5)

    def load(g, row):
        return in_ref[g, row : row + 8, :]

    copies = []
    for third in range(3):
        rows = slice(32 * third, 32 * third + 32)
        for j, (re, im) in enumerate(y_third(load, third, table_ref, twiddle_ref, lane_roll)):
            lanes = slice(WAVES * j, WAVES * (j + 1))
            s_re, s_im = real_ref[0, rows, lanes], imag_ref[0, rows, lanes]
            re, im = scale * re, scale * im
            out_re_ref[0, rows, lanes] = s_re * re - s_im * im
            out_im_ref[0, rows, lanes] = s_re * im + s_im * re
        for i, (source, target) in enumerate(((out_re_ref, out_re_hbm), (out_im_ref, out_im_hbm))):
            copies.append(
                pltpu.make_async_copy(
                    source.at[:, rows, :], target.at[:, rows, :], sems.at[2 * third + i]
                )
            )
            copies[-1].start()
    for copy in copies:
        copy.wait()


PARAMS = pltpu.CompilerParams(vmem_limit_bytes=24 * 1024 * 1024)


def exchange(sent, axis, order):
    return lax.all_to_all(
        sent, axis, split_axis=0, concat_axis=0, tiled=True, axis_index_groups=[order]
    )


def in_hbm(array):
    return pltpu.with_memory_space_constraint(array, pltpu.HBM)


def on_device(line_values, line_ids, line_start, line_stop, spectrum_real, spectrum_imag):
    z_table = jnp.asarray(wave_tables(KX_ORDER))
    y_table = jnp.asarray(wave_tables(range(64)))
    twiddle = jnp.asarray(twiddles())
    hbm = pl.BlockSpec(memory_space=pltpu.HBM)
    vmem = pl.BlockSpec(memory_space=pltpu.VMEM)
    sent = pl.pallas_call(
        x_kernel,
        out_shape=jax.ShapeDtypeStruct((KXW, 1, 2 * LINES_HERE), F32),
        in_specs=[hbm] * 5,
        out_specs=vmem,
        scratch_shapes=[
            pltpu.VMEM((1, LCAP), jnp.int32),
            pltpu.VMEM((1, LCAP), jnp.int32),
            pltpu.VMEM((1, LCAP), jnp.int32),
            pltpu.VMEM((LCAP, 2 * NG), F32),
            pltpu.VMEM((NG, 4 * KXW), BF16),
            pltpu.SemaphoreType.DMA((5,)),
        ],
        compiler_params=PARAMS,
        name="x_lines",
    )(
        in_hbm(line_ids.reshape(1, LCAP)),
        in_hbm(line_start.reshape(1, LCAP)),
        in_hbm(line_stop.reshape(1, LCAP)),
        in_hbm(line_values),
        in_hbm(jnp.asarray(x_tables())),
    )
    arrived = exchange(sent, "kx", KX_ORDER)
    sent = pl.pallas_call(
        z_kernel,
        out_shape=jax.ShapeDtypeStruct((GY, 72, 128), F32),
        compiler_params=PARAMS,
        name="z_rows",
    )(arrived, z_table, twiddle)
    arrived = exchange(sent, "gy", GY_ORDER)
    out = jax.ShapeDtypeStruct(spectrum_real.shape, F32)
    return pl.pallas_call(
        y_kernel,
        out_shape=(out, out),
        in_specs=[vmem] * 5,
        out_specs=(hbm, hbm),
        scratch_shapes=[
            pltpu.VMEM(spectrum_real.shape, F32),
            pltpu.VMEM(spectrum_real.shape, F32),
            pltpu.SemaphoreType.DMA((6,)),
        ],
        compiler_params=PARAMS,
        name="y_rows",
    )(arrived, spectrum_real, spectrum_imag, y_table, twiddle)


def solution(mesh):
    in_specs = (
        P(("kx", "gy"), None),
        P(("kx", "gy")),
        P(("kx", "gy")),
        P(("kx", "gy")),
        P("kx", "gy", None),
        P("kx", "gy", None),
    )
    out_specs = (P("kx", "gy", None), P("kx", "gy", None))
    return jax.shard_map(
        on_device, mesh=mesh, in_specs=in_specs, out_specs=out_specs, check_vma=False
    )
```

```python
import functools
import math

import jax
import jax.numpy as jnp
import ml_dtypes
import numpy as np
from jax import lax
from jax.experimental import pallas as pl
from jax.experimental.pallas import tpu as pltpu
from jax.sharding import PartitionSpec as P

NG = 384
BLK = 64
KXW = 64
YD = 48
ZD = 6
LCAP = 144
GY = 8
LINES_HERE = YD * ZD
WAVES = 128
F32 = jnp.float32
BF16 = jnp.bfloat16


KX_ORDER = [
    ((z + 7) % 8) * 8 + ((x + 2) % 4) * 2 + 1 - core
    for z in range(8)
    for x in range(4)
    for core in range(2)
]
GY_ORDER = [(y + 5) % GY for y in range(GY)]


def split(table):
    high = table.astype(np.float32).astype(ml_dtypes.bfloat16)
    low = (table - high.astype(np.float64)).astype(np.float32).astype(ml_dtypes.bfloat16)
    return high, low


def angles(first, second, length):
    return 2.0 * math.pi * ((first[:, None] * second[None, :]) % length) / length


def x_tables():
    angle = angles(np.arange(NG), np.array(KX_ORDER), 2 * NG)
    return np.concatenate(split(np.concatenate([np.cos(angle), np.sin(angle)], axis=1)), axis=1)


def wave_tables(order):
    angle = angles(np.array(order), np.arange(WAVES), WAVES)
    c, s = np.cos(angle), np.sin(angle)
    high, low = split(np.block([[c, -s], [s, c]]))
    return np.concatenate([high, high, low], axis=0)


def twiddles():
    angle = angles(np.arange(6), np.arange(WAVES), 2 * NG)
    both = np.zeros((16, WAVES), np.float32)
    both[0:6] = np.cos(angle)
    both[8:14] = np.sin(angle)
    return both


def halves(values):
    high = values.astype(BF16)
    low = (values - high.astype(F32)).astype(BF16)
    return high, low


def dot(a, b):
    return jnp.dot(a, b, preferred_element_type=F32)


def dft3(v0, v1, v2):
    s3 = math.sqrt(3.0) / 2.0
    sum_re, sum_im = v1[0] + v2[0], v1[1] + v2[1]
    dif_re, dif_im = s3 * (v1[0] - v2[0]), s3 * (v1[1] - v2[1])
    mid_re, mid_im = v0[0] - 0.5 * sum_re, v0[1] - 0.5 * sum_im
    return (
        (v0[0] + sum_re, v0[1] + sum_im),
        (mid_re + dif_im, mid_im - dif_re),
        (mid_re - dif_im, mid_im + dif_re),
    )


def dft6(v):
    s3 = math.sqrt(3.0) / 2.0
    even = dft3(v[0], v[2], v[4])
    odd = dft3(v[1], v[3], v[5])
    turned = (
        odd[0],
        (0.5 * odd[1][0] + s3 * odd[1][1], 0.5 * odd[1][1] - s3 * odd[1][0]),
        (-0.5 * odd[2][0] + s3 * odd[2][1], -0.5 * odd[2][1] - s3 * odd[2][0]),
    )
    front = [(e[0] + o[0], e[1] + o[1]) for e, o in zip(even, turned)]
    back = [(e[0] - o[0], e[1] - o[1]) for e, o in zip(even, turned)]
    return front + back


def waves(rows, table_ref):
    high, low = halves(rows)
    both = jnp.concatenate([high, low], axis=1)
    return dot(both, table_ref[0:256]) + dot(high, table_ref[256:384])


def twisted(wave_rows, rows, twiddle_ref):
    terms = []
    for u in range(6):
        re = wave_rows[u * rows : (u + 1) * rows, 0:WAVES]
        im = wave_rows[u * rows : (u + 1) * rows, WAVES : 2 * WAVES]
        if u > 0:
            c, s = twiddle_ref[u : u + 1, :], twiddle_ref[8 + u : 9 + u, :]
            re, im = re * c + im * s, im * c - re * s
        terms.append((re, im))
    return dft6(terms)


def quotient(values, divisor):
    return jnp.floor((values + 0.5) * (1.0 / divisor))


def lines_of(ids):
    ids = ids.astype(F32)
    y = quotient(ids, NG)
    z = ids - NG * y
    z_here = z - ZD * quotient(z, ZD)
    y_here = y - YD * quotient(y, YD)
    t = quotient(y_here, 6)
    target = z_here * YD + (y_here - 6.0 * t) * 8.0 + t
    target = jnp.where(ids < 0, -1.0, target).astype(jnp.int32)
    place = lax.broadcasted_iota(jnp.int32, (LINES_HERE, LCAP), 0)
    return jnp.where(place == target, 1.0, 0.0).astype(BF16)


def cells_of(start, stop):
    rows = [start.astype(F32) * BLK, stop.astype(F32) * BLK, jnp.zeros((6, LCAP), F32)]
    rows = jnp.concatenate(rows, axis=0)
    rows = jnp.concatenate([rows, jnp.zeros((8, 256 - LCAP), F32)], axis=1)
    columns = rows.T[0:LCAP].astype(jnp.int32)
    return columns[:, 0:1], columns[:, 1:2]


def x_body(start, stop, chosen, values, table, roll):
    position = lax.broadcasted_iota(jnp.int32, (LCAP, NG), 1)
    inside = (position >= start) & (position < stop)
    real = jnp.where(inside, values[:, 0:NG], 0.0)
    imag = jnp.where(inside, values[:, NG : 2 * NG], 0.0)
    high, low = halves(jnp.concatenate([real, imag], axis=0))
    sums = dot(jnp.concatenate([high, low], axis=0), table)
    sums = sums[:, 0 : 2 * KXW] + sums[:, 2 * KXW : 4 * KXW]
    sums = sums[0 : 2 * LCAP] + sums[2 * LCAP : 4 * LCAP]
    lane = lax.broadcasted_iota(jnp.int32, (LCAP, 2 * KXW), 1)
    real = sums[0:LCAP]
    spectrum = jnp.where(lane < KXW, real, -real) + roll(sums[LCAP : 2 * LCAP], KXW)
    placed = dot(chosen, jnp.concatenate(halves(spectrum), axis=1))
    placed = placed[:, 0 : 2 * KXW] + placed[:, 2 * KXW : 4 * KXW]
    placed = jnp.concatenate([placed, jnp.zeros((384 - LINES_HERE, 2 * KXW), F32)], axis=0).T
    real, imag = placed[0:KXW], placed[KXW : 2 * KXW]
    rest = LINES_HERE - 256
    lane = lax.broadcasted_iota(jnp.int32, (KXW, 128), 1)
    last = jnp.where(lane < rest, real[:, 256:384], roll(imag[:, 256:384], rest))
    return jnp.concatenate([real[:, 0:256], imag[:, 0:256], last[:, 0 : 2 * rest]], axis=1)


def x_kernel(
    ids_hbm, start_hbm, stop_hbm, values_hbm, table_hbm, out_ref,
    ids_ref, start_ref, stop_ref, values_ref, table_ref, sems,
):
    pairs = [
        (ids_hbm, ids_ref),
        (start_hbm, start_ref),
        (stop_hbm, stop_ref),
        (values_hbm, values_ref),
        (table_hbm, table_ref),
    ]
    copies = [
        pltpu.make_async_copy(source, target, sems.at[i])
        for i, (source, target) in enumerate(pairs)
    ]
    for copy in copies:
        copy.start()
    for copy in copies[0:3]:
        copy.wait()
    chosen = lines_of(ids_ref[...])
    start, stop = cells_of(start_ref[...], stop_ref[...])
    copies[4].wait()
    copies[3].wait()
    out_ref[:, 0, :] = x_body(
        start, stop, chosen, values_ref[...], table_ref[...], lane_roll
    )


def swap_blocks(tiles, roll):
    lane = lax.broadcasted_iota(jnp.int32, tiles[0].shape, 1)
    low64 = lane < 64
    even32 = (lane // 32) % 2 == 0
    q0, q1, q2, q3 = tiles
    q0, q2 = jnp.where(low64, q0, roll(q2, 64)), jnp.where(low64, roll(q0, 64), q2)
    q1, q3 = jnp.where(low64, q1, roll(q3, 64)), jnp.where(low64, roll(q1, 64), q3)
    q0, q1 = jnp.where(even32, q0, roll(q1, 32)), jnp.where(even32, roll(q0, 96), q1)
    q2, q3 = jnp.where(even32, q2, roll(q3, 32)), jnp.where(even32, roll(q2, 96), q3)
    return q0, q1, q2, q3


def lane_roll(values, shift):
    return pltpu.roll(values, shift, 1)


def z_body(arrived, table_ref, twiddle_ref, store, roll):
    rest = LINES_HERE - 256
    last = jnp.concatenate([arrived[:, 512:576], jnp.zeros((KXW, 64), F32)], axis=1)
    real = [arrived[:, 0:128], arrived[:, 128:256], last]
    imag = [arrived[:, 256:384], arrived[:, 384:512], roll(last, 128 - rest)]
    rows = [jnp.concatenate(pair, axis=0).T for pair in zip(real, imag)]
    rows = jnp.concatenate([rows[0], rows[1], rows[2][0:rest]], axis=0)
    spectrum = waves(rows, table_ref)
    for j, (re, im) in enumerate(twisted(spectrum, YD, twiddle_ref)):
        tiles = swap_blocks((re[0:24], re[24:48], im[0:24], im[24:48]), roll)
        for a in range(4):
            piece = 4 * j + a
            store(GY_ORDER.index(piece // 3), piece % 3, tiles[a])


def z_kernel(in_ref, table_ref, twiddle_ref, out_ref):
    def store(block, third, tile):
        out_ref[block, third * 24 : third * 24 + 24, :] = tile

    z_body(in_ref[:, 0, :], table_ref, twiddle_ref, store, lane_roll)


def y_waves(load, third, table_ref, roll):
    pieces = {}
    for e in range(3):
        rows = jnp.concatenate(
            [load(GY_ORDER.index(g), third * 24 + e * 8) for g in range(GY)], axis=0
        )
        flipped = jnp.concatenate([rows, roll(rows, 64)], axis=0).T
        pieces[e] = flipped[0:32]
        pieces[3 + e] = flipped[32:64]
    return waves(jnp.concatenate([pieces[u] for u in range(6)], axis=0), table_ref)


def y_kernel(
    in_ref, real_ref, imag_ref, table_ref, twiddle_ref, out_re_hbm, out_im_hbm,
    out_re_ref, out_im_ref, sems,
):
    scale = float(NG) ** (-1.5)

    def load(g, row):
        return in_ref[g, row : row + 8, :]

    copies = []
    spectrum = y_waves(load, 0, table_ref, lane_roll)
    for third in range(3):
        rows = slice(32 * third, 32 * third + 32)
        here = spectrum
        if third < 2:
            spectrum = y_waves(load, third + 1, table_ref, lane_roll)
        for j, (re, im) in enumerate(twisted(here, 32, twiddle_ref)):
            lanes = slice(WAVES * j, WAVES * (j + 1))
            s_re, s_im = real_ref[0, rows, lanes], imag_ref[0, rows, lanes]
            re, im = scale * re, scale * im
            out_re_ref[0, rows, lanes] = s_re * re - s_im * im
            out_im_ref[0, rows, lanes] = s_re * im + s_im * re
        for i, (source, target) in enumerate(((out_re_ref, out_re_hbm), (out_im_ref, out_im_hbm))):
            copies.append(
                pltpu.make_async_copy(
                    source.at[:, rows, :], target.at[:, rows, :], sems.at[2 * third + i]
                )
            )
            copies[-1].start()
    for copy in copies:
        copy.wait()


PARAMS = pltpu.CompilerParams(vmem_limit_bytes=24 * 1024 * 1024)


def exchange(sent, axis, order):
    return lax.all_to_all(
        sent, axis, split_axis=0, concat_axis=0, tiled=True, axis_index_groups=[order]
    )


def in_hbm(array):
    return pltpu.with_memory_space_constraint(array, pltpu.HBM)


def on_device(line_values, line_ids, line_start, line_stop, spectrum_real, spectrum_imag):
    z_table = jnp.asarray(wave_tables(KX_ORDER))
    y_table = jnp.asarray(wave_tables(range(64)))
    twiddle = jnp.asarray(twiddles())
    hbm = pl.BlockSpec(memory_space=pltpu.HBM)
    vmem = pl.BlockSpec(memory_space=pltpu.VMEM)
    sent = pl.pallas_call(
        x_kernel,
        out_shape=jax.ShapeDtypeStruct((KXW, 1, 2 * LINES_HERE), F32),
        in_specs=[hbm] * 5,
        out_specs=vmem,
        scratch_shapes=[
            pltpu.VMEM((1, LCAP), jnp.int32),
            pltpu.VMEM((1, LCAP), jnp.int32),
            pltpu.VMEM((1, LCAP), jnp.int32),
            pltpu.VMEM((LCAP, 2 * NG), F32),
            pltpu.VMEM((NG, 4 * KXW), BF16),
            pltpu.SemaphoreType.DMA((5,)),
        ],
        compiler_params=PARAMS,
        name="x_lines",
    )(
        in_hbm(line_ids.reshape(1, LCAP)),
        in_hbm(line_start.reshape(1, LCAP)),
        in_hbm(line_stop.reshape(1, LCAP)),
        in_hbm(line_values),
        in_hbm(jnp.asarray(x_tables())),
    )
    arrived = exchange(sent, "kx", KX_ORDER)
    sent = pl.pallas_call(
        z_kernel,
        out_shape=jax.ShapeDtypeStruct((GY, 72, 128), F32),
        compiler_params=PARAMS,
        name="z_rows",
    )(arrived, z_table, twiddle)
    arrived = exchange(sent, "gy", GY_ORDER)
    out = jax.ShapeDtypeStruct(spectrum_real.shape, F32)
    return pl.pallas_call(
        y_kernel,
        out_shape=(out, out),
        in_specs=[vmem] * 5,
        out_specs=(hbm, hbm),
        scratch_shapes=[
            pltpu.VMEM(spectrum_real.shape, F32),
            pltpu.VMEM(spectrum_real.shape, F32),
            pltpu.SemaphoreType.DMA((6,)),
        ],
        compiler_params=PARAMS,
        name="y_rows",
    )(arrived, spectrum_real, spectrum_imag, y_table, twiddle)


def solution(mesh):
    in_specs = (
        P(("kx", "gy"), None),
        P(("kx", "gy")),
        P(("kx", "gy")),
        P(("kx", "gy")),
        P("kx", "gy", None),
        P("kx", "gy", None),
    )
    out_specs = (P("kx", "gy", None), P("kx", "gy", None))
    return jax.shard_map(
        on_device, mesh=mesh, in_specs=in_specs, out_specs=out_specs, check_vma=False
    )
```

```python
import functools
import math

import jax
import jax.numpy as jnp
import ml_dtypes
import numpy as np
from jax import lax
from jax.experimental import pallas as pl
from jax.experimental.pallas import tpu as pltpu
from jax.sharding import PartitionSpec as P

NG = 384
BLK = 64
KXW = 64
YD = 48
ZD = 6
LCAP = 144
GY = 8
LINES_HERE = YD * ZD
WAVES = 128
F32 = jnp.float32
BF16 = jnp.bfloat16


KX_ORDER = [
    ((z + 7) % 8) * 8 + ((x + 2) % 4) * 2 + 1 - core
    for z in range(8)
    for x in range(4)
    for core in range(2)
]
GY_ORDER = [(y + 5) % GY for y in range(GY)]


def split(table):
    high = table.astype(np.float32).astype(ml_dtypes.bfloat16)
    low = (table - high.astype(np.float64)).astype(np.float32).astype(ml_dtypes.bfloat16)
    return high, low


def angles(first, second, length):
    return 2.0 * math.pi * ((first[:, None] * second[None, :]) % length) / length


def x_tables():
    angle = angles(np.arange(NG), np.array(KX_ORDER), 2 * NG)
    return np.concatenate(split(np.concatenate([np.cos(angle), np.sin(angle)], axis=1)), axis=1)


def wave_tables(order, scale=1.0):
    angle = angles(np.array(order), np.arange(WAVES), WAVES)
    c, s = scale * np.cos(angle), scale * np.sin(angle)
    high, low = split(np.block([[c, -s], [s, c]]))
    return np.concatenate([high, high, low], axis=0)


def twiddles():
    angle = angles(np.arange(6), np.arange(WAVES), 2 * NG)
    both = np.zeros((16, WAVES), np.float32)
    both[0:6] = np.cos(angle)
    both[8:14] = np.sin(angle)
    return both


def halves(values):
    high = values.astype(BF16)
    low = (values - high.astype(F32)).astype(BF16)
    return high, low


def dot(a, b):
    return jnp.dot(a, b, preferred_element_type=F32)


def dft3(v0, v1, v2):
    s3 = math.sqrt(3.0) / 2.0
    sum_re, sum_im = v1[0] + v2[0], v1[1] + v2[1]
    dif_re, dif_im = s3 * (v1[0] - v2[0]), s3 * (v1[1] - v2[1])
    mid_re, mid_im = v0[0] - 0.5 * sum_re, v0[1] - 0.5 * sum_im
    return (
        (v0[0] + sum_re, v0[1] + sum_im),
        (mid_re + dif_im, mid_im - dif_re),
        (mid_re - dif_im, mid_im + dif_re),
    )


def dft6(v):
    s3 = math.sqrt(3.0) / 2.0
    even = dft3(v[0], v[2], v[4])
    odd = dft3(v[1], v[3], v[5])
    turned = (
        odd[0],
        (0.5 * odd[1][0] + s3 * odd[1][1], 0.5 * odd[1][1] - s3 * odd[1][0]),
        (-0.5 * odd[2][0] + s3 * odd[2][1], -0.5 * odd[2][1] - s3 * odd[2][0]),
    )
    front = [(e[0] + o[0], e[1] + o[1]) for e, o in zip(even, turned)]
    back = [(e[0] - o[0], e[1] - o[1]) for e, o in zip(even, turned)]
    return front + back


def waves(rows, table_ref):
    high, low = halves(rows)
    both = jnp.concatenate([high, low], axis=1)
    return dot(both, table_ref[0:256]) + dot(high, table_ref[256:384])


def twisted(wave_rows, rows, twiddle_ref):
    terms = []
    for u in range(6):
        re = wave_rows[u * rows : (u + 1) * rows, 0:WAVES]
        im = wave_rows[u * rows : (u + 1) * rows, WAVES : 2 * WAVES]
        if u > 0:
            c, s = twiddle_ref[u : u + 1, :], twiddle_ref[8 + u : 9 + u, :]
            re, im = re * c + im * s, im * c - re * s
        terms.append((re, im))
    return dft6(terms)


def quotient(values, divisor):
    return jnp.floor((values + 0.5) * (1.0 / divisor))


def lines_of(ids):
    ids = ids.astype(F32)
    y = quotient(ids, NG)
    z = ids - NG * y
    z_here = z - ZD * quotient(z, ZD)
    y_here = y - YD * quotient(y, YD)
    t = quotient(y_here, 6)
    target = z_here * YD + (y_here - 6.0 * t) * 8.0 + t
    target = jnp.where(ids < 0, -1.0, target).astype(jnp.int32)
    place = lax.broadcasted_iota(jnp.int32, (LINES_HERE, LCAP), 0)
    return jnp.where(place == target, 1.0, 0.0).astype(BF16)


def cells_of(start, stop):
    rows = [start.astype(F32) * BLK, stop.astype(F32) * BLK, jnp.zeros((6, LCAP), F32)]
    rows = jnp.concatenate(rows, axis=0)
    rows = jnp.concatenate([rows, jnp.zeros((8, 256 - LCAP), F32)], axis=1)
    columns = rows.T[0:LCAP].astype(jnp.int32)
    return columns[:, 0:1], columns[:, 1:2]


def x_body(start, stop, chosen, values, table, roll):
    position = lax.broadcasted_iota(jnp.int32, (LCAP, NG), 1)
    inside = (position >= start) & (position < stop)
    real = jnp.where(inside, values[:, 0:NG], 0.0)
    imag = jnp.where(inside, values[:, NG : 2 * NG], 0.0)
    high, low = halves(jnp.concatenate([real, imag], axis=0))
    sums = dot(jnp.concatenate([high, low], axis=0), table)
    sums = sums[:, 0 : 2 * KXW] + sums[:, 2 * KXW : 4 * KXW]
    sums = sums[0 : 2 * LCAP] + sums[2 * LCAP : 4 * LCAP]
    lane = lax.broadcasted_iota(jnp.int32, (LCAP, 2 * KXW), 1)
    real = sums[0:LCAP]
    spectrum = jnp.where(lane < KXW, real, -real) + roll(sums[LCAP : 2 * LCAP], KXW)
    placed = dot(chosen, jnp.concatenate(halves(spectrum), axis=1))
    placed = placed[:, 0 : 2 * KXW] + placed[:, 2 * KXW : 4 * KXW]
    placed = jnp.concatenate([placed, jnp.zeros((384 - LINES_HERE, 2 * KXW), F32)], axis=0).T
    real, imag = placed[0:KXW], placed[KXW : 2 * KXW]
    rest = LINES_HERE - 256
    lane = lax.broadcasted_iota(jnp.int32, (KXW, 128), 1)
    last = jnp.where(lane < rest, real[:, 256:384], roll(imag[:, 256:384], rest))
    return jnp.concatenate([real[:, 0:256], imag[:, 0:256], last[:, 0 : 2 * rest]], axis=1)


def x_kernel(
    ids_hbm, start_hbm, stop_hbm, values_hbm, table_hbm, out_ref,
    ids_ref, start_ref, stop_ref, values_ref, table_ref, sems,
):
    pairs = [
        (values_hbm, values_ref),
        (table_hbm, table_ref),
        (ids_hbm, ids_ref),
        (start_hbm, start_ref),
        (stop_hbm, stop_ref),
    ]
    copies = [
        pltpu.make_async_copy(source, target, sems.at[i])
        for i, (source, target) in enumerate(pairs)
    ]
    for copy in copies:
        copy.start()
    for copy in copies[2:5]:
        copy.wait()
    chosen = lines_of(ids_ref[...])
    start, stop = cells_of(start_ref[...], stop_ref[...])
    copies[1].wait()
    copies[0].wait()
    out_ref[:, 0, :] = x_body(
        start, stop, chosen, values_ref[...], table_ref[...], lane_roll
    )


def swap_blocks(tiles, roll):
    lane = lax.broadcasted_iota(jnp.int32, tiles[0].shape, 1)
    low64 = lane < 64
    even32 = (lane // 32) % 2 == 0
    q0, q1, q2, q3 = tiles
    q0, q2 = jnp.where(low64, q0, roll(q2, 64)), jnp.where(low64, roll(q0, 64), q2)
    q1, q3 = jnp.where(low64, q1, roll(q3, 64)), jnp.where(low64, roll(q1, 64), q3)
    q0, q1 = jnp.where(even32, q0, roll(q1, 32)), jnp.where(even32, roll(q0, 96), q1)
    q2, q3 = jnp.where(even32, q2, roll(q3, 32)), jnp.where(even32, roll(q2, 96), q3)
    return q0, q1, q2, q3


def lane_roll(values, shift):
    return pltpu.roll(values, shift, 1)


def z_body(arrived, table_ref, twiddle_ref, store, roll):
    rest = LINES_HERE - 256
    last = jnp.concatenate([arrived[:, 512:576], jnp.zeros((KXW, 64), F32)], axis=1)
    real = [arrived[:, 0:128], arrived[:, 128:256], last]
    imag = [arrived[:, 256:384], arrived[:, 384:512], roll(last, 128 - rest)]
    rows = [jnp.concatenate(pair, axis=0).T for pair in zip(real, imag)]
    rows = jnp.concatenate([rows[0], rows[1], rows[2][0:rest]], axis=0)
    spectrum = waves(rows, table_ref)
    for j, (re, im) in enumerate(twisted(spectrum, YD, twiddle_ref)):
        tiles = swap_blocks((re[0:24], re[24:48], im[0:24], im[24:48]), roll)
        for a in range(4):
            piece = 4 * j + a
            store(GY_ORDER.index(piece // 3), piece % 3, tiles[a])


def z_kernel(in_ref, table_ref, twiddle_ref, out_ref):
    def store(block, third, tile):
        out_ref[block, third * 24 : third * 24 + 24, :] = tile

    z_body(in_ref[:, 0, :], table_ref, twiddle_ref, store, lane_roll)


def y_waves(load, third, table_ref, roll):
    pieces = {}
    for e in range(3):
        rows = jnp.concatenate(
            [load(GY_ORDER.index(g), third * 24 + e * 8) for g in range(GY)], axis=0
        )
        flipped = jnp.concatenate([rows, roll(rows, 64)], axis=0).T
        pieces[e] = flipped[0:32]
        pieces[3 + e] = flipped[32:64]
    return waves(jnp.concatenate([pieces[u] for u in range(6)], axis=0), table_ref)


def y_kernel(
    in_ref, real_ref, imag_ref, table_ref, twiddle_ref, out_re_hbm, out_im_hbm,
    out_re_ref, out_im_ref, sems,
):
    def load(g, row):
        return in_ref[g, row : row + 8, :]

    copies = []
    spectrum = y_waves(load, 0, table_ref, lane_roll)
    for third in range(3):
        rows = slice(32 * third, 32 * third + 32)
        here = spectrum
        if third < 2:
            spectrum = y_waves(load, third + 1, table_ref, lane_roll)
        for j, (re, im) in enumerate(twisted(here, 32, twiddle_ref)):
            lanes = slice(WAVES * j, WAVES * (j + 1))
            s_re, s_im = real_ref[0, rows, lanes], imag_ref[0, rows, lanes]
            out_re_ref[0, rows, lanes] = s_re * re - s_im * im
            out_im_ref[0, rows, lanes] = s_re * im + s_im * re
        for i, (source, target) in enumerate(((out_re_ref, out_re_hbm), (out_im_ref, out_im_hbm))):
            copies.append(
                pltpu.make_async_copy(
                    source.at[:, rows, :], target.at[:, rows, :], sems.at[2 * third + i]
                )
            )
            copies[-1].start()
    for copy in copies:
        copy.wait()


PARAMS = pltpu.CompilerParams(vmem_limit_bytes=24 * 1024 * 1024)


def exchange(sent, axis, order):
    return lax.all_to_all(
        sent, axis, split_axis=0, concat_axis=0, tiled=True, axis_index_groups=[order]
    )


def in_hbm(array):
    return pltpu.with_memory_space_constraint(array, pltpu.HBM)


def on_device(line_values, line_ids, line_start, line_stop, spectrum_real, spectrum_imag):
    z_table = jnp.asarray(wave_tables(KX_ORDER))
    y_table = jnp.asarray(wave_tables(range(64), float(NG) ** (-1.5)))
    twiddle = jnp.asarray(twiddles())
    hbm = pl.BlockSpec(memory_space=pltpu.HBM)
    vmem = pl.BlockSpec(memory_space=pltpu.VMEM)
    sent = pl.pallas_call(
        x_kernel,
        out_shape=jax.ShapeDtypeStruct((KXW, 1, 2 * LINES_HERE), F32),
        in_specs=[hbm] * 5,
        out_specs=vmem,
        scratch_shapes=[
            pltpu.VMEM((1, LCAP), jnp.int32),
            pltpu.VMEM((1, LCAP), jnp.int32),
            pltpu.VMEM((1, LCAP), jnp.int32),
            pltpu.VMEM((LCAP, 2 * NG), F32),
            pltpu.VMEM((NG, 4 * KXW), BF16),
            pltpu.SemaphoreType.DMA((5,)),
        ],
        compiler_params=PARAMS,
        name="x_lines",
    )(
        in_hbm(line_ids.reshape(1, LCAP)),
        in_hbm(line_start.reshape(1, LCAP)),
        in_hbm(line_stop.reshape(1, LCAP)),
        in_hbm(line_values),
        in_hbm(jnp.asarray(x_tables())),
    )
    arrived = exchange(sent, "kx", KX_ORDER)
    sent = pl.pallas_call(
        z_kernel,
        out_shape=jax.ShapeDtypeStruct((GY, 72, 128), F32),
        compiler_params=PARAMS,
        name="z_rows",
    )(arrived, z_table, twiddle)
    arrived = exchange(sent, "gy", GY_ORDER)
    out = jax.ShapeDtypeStruct(spectrum_real.shape, F32)
    return pl.pallas_call(
        y_kernel,
        out_shape=(out, out),
        in_specs=[vmem] * 5,
        out_specs=(hbm, hbm),
        scratch_shapes=[
            pltpu.VMEM(spectrum_real.shape, F32),
            pltpu.VMEM(spectrum_real.shape, F32),
            pltpu.SemaphoreType.DMA((6,)),
        ],
        compiler_params=PARAMS,
        name="y_rows",
    )(arrived, spectrum_real, spectrum_imag, y_table, twiddle)


def solution(mesh):
    in_specs = (
        P(("kx", "gy"), None),
        P(("kx", "gy")),
        P(("kx", "gy")),
        P(("kx", "gy")),
        P("kx", "gy", None),
        P("kx", "gy", None),
    )
    out_specs = (P("kx", "gy", None), P("kx", "gy", None))
    return jax.shard_map(
        on_device, mesh=mesh, in_specs=in_specs, out_specs=out_specs, check_vma=False
    )
```

```python
import functools
import math

import jax
import jax.numpy as jnp
import ml_dtypes
import numpy as np
from jax import lax
from jax.experimental import pallas as pl
from jax.experimental.pallas import tpu as pltpu
from jax.sharding import PartitionSpec as P

NG = 384
BLK = 64
KXW = 64
YD = 48
ZD = 6
LCAP = 144
GY = 8
LINES_HERE = YD * ZD
WAVES = 128
F32 = jnp.float32
BF16 = jnp.bfloat16


KX_ORDER = [
    ((z + 7) % 8) * 8 + ((2 - x) % 4) * 2 + 1 - core
    for z in range(8)
    for x in range(4)
    for core in range(2)
]
GY_ORDER = [(y + 5) % GY for y in range(GY)]


def split(table):
    high = table.astype(np.float32).astype(ml_dtypes.bfloat16)
    low = (table - high.astype(np.float64)).astype(np.float32).astype(ml_dtypes.bfloat16)
    return high, low


def angles(first, second, length):
    return 2.0 * math.pi * ((first[:, None] * second[None, :]) % length) / length


def x_tables():
    angle = angles(np.arange(NG), np.array(KX_ORDER), 2 * NG)
    return np.concatenate(split(np.concatenate([np.cos(angle), np.sin(angle)], axis=1)), axis=1)


def wave_tables(order, scale=1.0):
    angle = angles(np.array(order), np.arange(WAVES), WAVES)
    c, s = scale * np.cos(angle), scale * np.sin(angle)
    high, low = split(np.block([[c, -s], [s, c]]))
    return np.concatenate([high, high, low], axis=0)


def twiddles():
    angle = angles(np.arange(6), np.arange(WAVES), 2 * NG)
    both = np.zeros((16, WAVES), np.float32)
    both[0:6] = np.cos(angle)
    both[8:14] = np.sin(angle)
    return both


def halves(values):
    high = values.astype(BF16)
    low = (values - high.astype(F32)).astype(BF16)
    return high, low


def dot(a, b):
    return jnp.dot(a, b, preferred_element_type=F32)


def dft3(v0, v1, v2):
    s3 = math.sqrt(3.0) / 2.0
    sum_re, sum_im = v1[0] + v2[0], v1[1] + v2[1]
    dif_re, dif_im = s3 * (v1[0] - v2[0]), s3 * (v1[1] - v2[1])
    mid_re, mid_im = v0[0] - 0.5 * sum_re, v0[1] - 0.5 * sum_im
    return (
        (v0[0] + sum_re, v0[1] + sum_im),
        (mid_re + dif_im, mid_im - dif_re),
        (mid_re - dif_im, mid_im + dif_re),
    )


def dft6(v):
    s3 = math.sqrt(3.0) / 2.0
    even = dft3(v[0], v[2], v[4])
    odd = dft3(v[1], v[3], v[5])
    turned = (
        odd[0],
        (0.5 * odd[1][0] + s3 * odd[1][1], 0.5 * odd[1][1] - s3 * odd[1][0]),
        (-0.5 * odd[2][0] + s3 * odd[2][1], -0.5 * odd[2][1] - s3 * odd[2][0]),
    )
    front = [(e[0] + o[0], e[1] + o[1]) for e, o in zip(even, turned)]
    back = [(e[0] - o[0], e[1] - o[1]) for e, o in zip(even, turned)]
    return front + back


def waves(rows, table_ref):
    high, low = halves(rows)
    both = jnp.concatenate([high, low], axis=1)
    return dot(both, table_ref[0:256]) + dot(high, table_ref[256:384])


def twisted(wave_rows, rows, twiddle_ref):
    terms = []
    for u in range(6):
        re = wave_rows[u * rows : (u + 1) * rows, 0:WAVES]
        im = wave_rows[u * rows : (u + 1) * rows, WAVES : 2 * WAVES]
        if u > 0:
            c, s = twiddle_ref[u : u + 1, :], twiddle_ref[8 + u : 9 + u, :]
            re, im = re * c + im * s, im * c - re * s
        terms.append((re, im))
    return dft6(terms)


def quotient(values, divisor):
    return jnp.floor((values + 0.5) * (1.0 / divisor))


def lines_of(ids):
    ids = ids.astype(F32)
    y = quotient(ids, NG)
    z = ids - NG * y
    z_here = z - ZD * quotient(z, ZD)
    y_here = y - YD * quotient(y, YD)
    t = quotient(y_here, 6)
    target = z_here * YD + (y_here - 6.0 * t) * 8.0 + t
    target = jnp.where(ids < 0, -1.0, target).astype(jnp.int32)
    place = lax.broadcasted_iota(jnp.int32, (LINES_HERE, LCAP), 0)
    return jnp.where(place == target, 1.0, 0.0).astype(BF16)


def cells_of(start, stop):
    rows = [start.astype(F32) * BLK, stop.astype(F32) * BLK, jnp.zeros((6, LCAP), F32)]
    rows = jnp.concatenate(rows, axis=0)
    rows = jnp.concatenate([rows, jnp.zeros((8, 256 - LCAP), F32)], axis=1)
    columns = rows.T[0:LCAP].astype(jnp.int32)
    return columns[:, 0:1], columns[:, 1:2]


def x_body(start, stop, chosen, values, table, roll):
    position = lax.broadcasted_iota(jnp.int32, (LCAP, NG), 1)
    inside = (position >= start) & (position < stop)
    real = jnp.where(inside, values[:, 0:NG], 0.0)
    imag = jnp.where(inside, values[:, NG : 2 * NG], 0.0)
    high, low = halves(jnp.concatenate([real, imag], axis=0))
    sums = dot(jnp.concatenate([high, low], axis=0), table)
    sums = sums[:, 0 : 2 * KXW] + sums[:, 2 * KXW : 4 * KXW]
    sums = sums[0 : 2 * LCAP] + sums[2 * LCAP : 4 * LCAP]
    lane = lax.broadcasted_iota(jnp.int32, (LCAP, 2 * KXW), 1)
    real = sums[0:LCAP]
    spectrum = jnp.where(lane < KXW, real, -real) + roll(sums[LCAP : 2 * LCAP], KXW)
    placed = dot(chosen, jnp.concatenate(halves(spectrum), axis=1))
    placed = placed[:, 0 : 2 * KXW] + placed[:, 2 * KXW : 4 * KXW]
    placed = jnp.concatenate([placed, jnp.zeros((384 - LINES_HERE, 2 * KXW), F32)], axis=0).T
    real, imag = placed[0:KXW], placed[KXW : 2 * KXW]
    rest = LINES_HERE - 256
    lane = lax.broadcasted_iota(jnp.int32, (KXW, 128), 1)
    last = jnp.where(lane < rest, real[:, 256:384], roll(imag[:, 256:384], rest))
    return jnp.concatenate([real[:, 0:256], imag[:, 0:256], last[:, 0 : 2 * rest]], axis=1)


def x_kernel(
    ids_hbm, start_hbm, stop_hbm, values_hbm, table_hbm, out_ref,
    ids_ref, start_ref, stop_ref, values_ref, table_ref, sems,
):
    pairs = [
        (values_hbm, values_ref),
        (table_hbm, table_ref),
        (ids_hbm, ids_ref),
        (start_hbm, start_ref),
        (stop_hbm, stop_ref),
    ]
    copies = [
        pltpu.make_async_copy(source, target, sems.at[i])
        for i, (source, target) in enumerate(pairs)
    ]
    for copy in copies:
        copy.start()
    copies[3].wait()
    copies[4].wait()
    start, stop = cells_of(start_ref[...], stop_ref[...])
    for copy in copies[0:3]:
        copy.wait()
    chosen = lines_of(ids_ref[...])
    out_ref[:, 0, :] = x_body(
        start, stop, chosen, values_ref[...], table_ref[...], lane_roll
    )


def swap_blocks(tiles, roll):
    lane = lax.broadcasted_iota(jnp.int32, tiles[0].shape, 1)
    low64 = lane < 64
    even32 = (lane // 32) % 2 == 0
    q0, q1, q2, q3 = tiles
    q0, q2 = jnp.where(low64, q0, roll(q2, 64)), jnp.where(low64, roll(q0, 64), q2)
    q1, q3 = jnp.where(low64, q1, roll(q3, 64)), jnp.where(low64, roll(q1, 64), q3)
    q0, q1 = jnp.where(even32, q0, roll(q1, 32)), jnp.where(even32, roll(q0, 96), q1)
    q2, q3 = jnp.where(even32, q2, roll(q3, 32)), jnp.where(even32, roll(q2, 96), q3)
    return q0, q1, q2, q3


def lane_roll(values, shift):
    return pltpu.roll(values, shift, 1)


def z_body(arrived, table_ref, twiddle_ref, store, roll):
    rest = LINES_HERE - 256
    last = jnp.concatenate([arrived[:, 512:576], jnp.zeros((KXW, 64), F32)], axis=1)
    real = [arrived[:, 0:128], arrived[:, 128:256], last]
    imag = [arrived[:, 256:384], arrived[:, 384:512], roll(last, 128 - rest)]
    rows = [jnp.concatenate(pair, axis=0).T for pair in zip(real, imag)]
    rows = jnp.concatenate([rows[0], rows[1], rows[2][0:rest]], axis=0)
    spectrum = waves(rows, table_ref)
    for j, (re, im) in enumerate(twisted(spectrum, YD, twiddle_ref)):
        tiles = swap_blocks((re[0:24], re[24:48], im[0:24], im[24:48]), roll)
        for a in range(4):
            piece = 4 * j + a
            store(GY_ORDER.index(piece // 3), piece % 3, tiles[a])


def z_kernel(in_ref, table_ref, twiddle_ref, out_ref):
    def store(block, third, tile):
        out_ref[block, third * 24 : third * 24 + 24, :] = tile

    z_body(in_ref[:, 0, :], table_ref, twiddle_ref, store, lane_roll)


def y_waves(load, third, table_ref, roll):
    pieces = {}
    for e in range(3):
        rows = jnp.concatenate(
            [load(GY_ORDER.index(g), third * 24 + e * 8) for g in range(GY)], axis=0
        )
        flipped = jnp.concatenate([rows, roll(rows, 64)], axis=0).T
        pieces[e] = flipped[0:32]
        pieces[3 + e] = flipped[32:64]
    return waves(jnp.concatenate([pieces[u] for u in range(6)], axis=0), table_ref)


def y_kernel(
    in_ref, real_ref, imag_ref, table_ref, twiddle_ref, out_re_hbm, out_im_hbm,
    out_re_ref, out_im_ref, sems,
):
    def load(g, row):
        return in_ref[g, row : row + 8, :]

    copies = []
    spectrum = y_waves(load, 0, table_ref, lane_roll)
    for third in range(3):
        rows = slice(32 * third, 32 * third + 32)
        here = spectrum
        if third < 2:
            spectrum = y_waves(load, third + 1, table_ref, lane_roll)
        for j, (re, im) in enumerate(twisted(here, 32, twiddle_ref)):
            lanes = slice(WAVES * j, WAVES * (j + 1))
            s_re, s_im = real_ref[0, rows, lanes], imag_ref[0, rows, lanes]
            out_re_ref[0, rows, lanes] = s_re * re - s_im * im
            out_im_ref[0, rows, lanes] = s_re * im + s_im * re
        for i, (source, target) in enumerate(((out_re_ref, out_re_hbm), (out_im_ref, out_im_hbm))):
            copies.append(
                pltpu.make_async_copy(
                    source.at[:, rows, :], target.at[:, rows, :], sems.at[2 * third + i]
                )
            )
            copies[-1].start()
    for copy in copies:
        copy.wait()


PARAMS = pltpu.CompilerParams(vmem_limit_bytes=24 * 1024 * 1024)


def exchange(sent, axis, order):
    return lax.all_to_all(
        sent, axis, split_axis=0, concat_axis=0, tiled=True, axis_index_groups=[order]
    )


def in_hbm(array):
    return pltpu.with_memory_space_constraint(array, pltpu.HBM)


def on_device(line_values, line_ids, line_start, line_stop, spectrum_real, spectrum_imag):
    z_table = jnp.asarray(wave_tables(KX_ORDER))
    y_table = jnp.asarray(wave_tables(range(64), float(NG) ** (-1.5)))
    twiddle = jnp.asarray(twiddles())
    hbm = pl.BlockSpec(memory_space=pltpu.HBM)
    vmem = pl.BlockSpec(memory_space=pltpu.VMEM)
    sent = pl.pallas_call(
        x_kernel,
        out_shape=jax.ShapeDtypeStruct((KXW, 1, 2 * LINES_HERE), F32),
        in_specs=[hbm] * 5,
        out_specs=vmem,
        scratch_shapes=[
            pltpu.VMEM((1, LCAP), jnp.int32),
            pltpu.VMEM((1, LCAP), jnp.int32),
            pltpu.VMEM((1, LCAP), jnp.int32),
            pltpu.VMEM((LCAP, 2 * NG), F32),
            pltpu.VMEM((NG, 4 * KXW), BF16),
            pltpu.SemaphoreType.DMA((5,)),
        ],
        compiler_params=PARAMS,
        name="x_lines",
    )(
        in_hbm(line_ids.reshape(1, LCAP)),
        in_hbm(line_start.reshape(1, LCAP)),
        in_hbm(line_stop.reshape(1, LCAP)),
        in_hbm(line_values),
        in_hbm(jnp.asarray(x_tables())),
    )
    arrived = exchange(sent, "kx", KX_ORDER)
    sent = pl.pallas_call(
        z_kernel,
        out_shape=jax.ShapeDtypeStruct((GY, 72, 128), F32),
        compiler_params=PARAMS,
        name="z_rows",
    )(arrived, z_table, twiddle)
    arrived = exchange(sent, "gy", GY_ORDER)
    out = jax.ShapeDtypeStruct(spectrum_real.shape, F32)
    return pl.pallas_call(
        y_kernel,
        out_shape=(out, out),
        in_specs=[vmem] * 5,
        out_specs=(hbm, hbm),
        scratch_shapes=[
            pltpu.VMEM(spectrum_real.shape, F32),
            pltpu.VMEM(spectrum_real.shape, F32),
            pltpu.SemaphoreType.DMA((6,)),
        ],
        compiler_params=PARAMS,
        name="y_rows",
    )(arrived, spectrum_real, spectrum_imag, y_table, twiddle)


def solution(mesh):
    in_specs = (
        P(("kx", "gy"), None),
        P(("kx", "gy")),
        P(("kx", "gy")),
        P(("kx", "gy")),
        P("kx", "gy", None),
        P("kx", "gy", None),
    )
    out_specs = (P("kx", "gy", None), P("kx", "gy", None))
    return jax.shard_map(
        on_device, mesh=mesh, in_specs=in_specs, out_specs=out_specs, check_vma=False
    )
```

```python
import functools
import math

import jax
import jax.numpy as jnp
import ml_dtypes
import numpy as np
from jax import lax
from jax.experimental import pallas as pl
from jax.experimental.pallas import tpu as pltpu
from jax.sharding import PartitionSpec as P

NG = 384
BLK = 64
KXW = 64
YD = 48
ZD = 6
LCAP = 144
GY = 8
LINES_HERE = YD * ZD
WAVES = 128
F32 = jnp.float32
BF16 = jnp.bfloat16


KX_ORDER = [
    ((z + 6) % 8) * 8 + ((2 - x) % 4) * 2 + 1 - core
    for z in range(8)
    for x in range(4)
    for core in range(2)
]
GY_ORDER = [(y + 5) % GY for y in range(GY)]


def split(table):
    high = table.astype(np.float32).astype(ml_dtypes.bfloat16)
    low = (table - high.astype(np.float64)).astype(np.float32).astype(ml_dtypes.bfloat16)
    return high, low


def angles(first, second, length):
    return 2.0 * math.pi * ((first[:, None] * second[None, :]) % length) / length


def x_tables():
    angle = angles(np.arange(NG), np.array(KX_ORDER), 2 * NG)
    return np.concatenate(split(np.concatenate([np.cos(angle), np.sin(angle)], axis=1)), axis=1)


def wave_tables(order, scale=1.0):
    angle = angles(np.array(order), np.arange(WAVES), WAVES)
    c, s = scale * np.cos(angle), scale * np.sin(angle)
    high, low = split(np.block([[c, -s], [s, c]]))
    return np.concatenate([high, high, low], axis=0)


def twiddles():
    angle = angles(np.arange(6), np.arange(WAVES), 2 * NG)
    both = np.zeros((16, WAVES), np.float32)
    both[0:6] = np.cos(angle)
    both[8:14] = np.sin(angle)
    return both


def halves(values):
    high = values.astype(BF16)
    low = (values - high.astype(F32)).astype(BF16)
    return high, low


def dot(a, b):
    return jnp.dot(a, b, preferred_element_type=F32)


def dft3(v0, v1, v2):
    s3 = math.sqrt(3.0) / 2.0
    sum_re, sum_im = v1[0] + v2[0], v1[1] + v2[1]
    dif_re, dif_im = s3 * (v1[0] - v2[0]), s3 * (v1[1] - v2[1])
    mid_re, mid_im = v0[0] - 0.5 * sum_re, v0[1] - 0.5 * sum_im
    return (
        (v0[0] + sum_re, v0[1] + sum_im),
        (mid_re + dif_im, mid_im - dif_re),
        (mid_re - dif_im, mid_im + dif_re),
    )


def dft6(v):
    s3 = math.sqrt(3.0) / 2.0
    even = dft3(v[0], v[2], v[4])
    odd = dft3(v[1], v[3], v[5])
    turned = (
        odd[0],
        (0.5 * odd[1][0] + s3 * odd[1][1], 0.5 * odd[1][1] - s3 * odd[1][0]),
        (-0.5 * odd[2][0] + s3 * odd[2][1], -0.5 * odd[2][1] - s3 * odd[2][0]),
    )
    front = [(e[0] + o[0], e[1] + o[1]) for e, o in zip(even, turned)]
    back = [(e[0] - o[0], e[1] - o[1]) for e, o in zip(even, turned)]
    return front + back


def waves(rows, table_ref):
    high, low = halves(rows)
    both = jnp.concatenate([high, low], axis=1)
    return dot(both, table_ref[0:256]) + dot(high, table_ref[256:384])


def twisted(wave_rows, rows, twiddle_ref):
    terms = []
    for u in range(6):
        re = wave_rows[u * rows : (u + 1) * rows, 0:WAVES]
        im = wave_rows[u * rows : (u + 1) * rows, WAVES : 2 * WAVES]
        if u > 0:
            c, s = twiddle_ref[u : u + 1, :], twiddle_ref[8 + u : 9 + u, :]
            re, im = re * c + im * s, im * c - re * s
        terms.append((re, im))
    return dft6(terms)


def quotient(values, divisor):
    return jnp.floor((values + 0.5) * (1.0 / divisor))


def lines_of(ids):
    ids = ids.astype(F32)
    y = quotient(ids, NG)
    z = ids - NG * y
    z_here = z - ZD * quotient(z, ZD)
    y_here = y - YD * quotient(y, YD)
    t = quotient(y_here, 6)
    target = z_here * YD + (y_here - 6.0 * t) * 8.0 + t
    target = jnp.where(ids < 0, -1.0, target).astype(jnp.int32)
    place = lax.broadcasted_iota(jnp.int32, (LINES_HERE, LCAP), 0)
    return jnp.where(place == target, 1.0, 0.0).astype(BF16)


def cells_of(start, stop):
    rows = [start.astype(F32) * BLK, stop.astype(F32) * BLK, jnp.zeros((6, LCAP), F32)]
    rows = jnp.concatenate(rows, axis=0)
    rows = jnp.concatenate([rows, jnp.zeros((8, 256 - LCAP), F32)], axis=1)
    columns = rows.T[0:LCAP].astype(jnp.int32)
    return columns[:, 0:1], columns[:, 1:2]


def x_body(start, stop, chosen, values, table, roll):
    position = lax.broadcasted_iota(jnp.int32, (LCAP, NG), 1)
    inside = (position >= start) & (position < stop)
    real = jnp.where(inside, values[:, 0:NG], 0.0)
    imag = jnp.where(inside, values[:, NG : 2 * NG], 0.0)
    high, low = halves(jnp.concatenate([real, imag], axis=0))
    sums = dot(jnp.concatenate([high, low], axis=0), table)
    sums = sums[:, 0 : 2 * KXW] + sums[:, 2 * KXW : 4 * KXW]
    sums = sums[0 : 2 * LCAP] + sums[2 * LCAP : 4 * LCAP]
    lane = lax.broadcasted_iota(jnp.int32, (LCAP, 2 * KXW), 1)
    real = sums[0:LCAP]
    spectrum = jnp.where(lane < KXW, real, -real) + roll(sums[LCAP : 2 * LCAP], KXW)
    placed = dot(chosen, jnp.concatenate(halves(spectrum), axis=1))
    placed = placed[:, 0 : 2 * KXW] + placed[:, 2 * KXW : 4 * KXW]
    placed = jnp.concatenate([placed, jnp.zeros((384 - LINES_HERE, 2 * KXW), F32)], axis=0).T
    real, imag = placed[0:KXW], placed[KXW : 2 * KXW]
    rest = LINES_HERE - 256
    lane = lax.broadcasted_iota(jnp.int32, (KXW, 128), 1)
    last = jnp.where(lane < rest, real[:, 256:384], roll(imag[:, 256:384], rest))
    return jnp.concatenate([real[:, 0:256], imag[:, 0:256], last[:, 0 : 2 * rest]], axis=1)


def x_kernel(
    ids_hbm, start_hbm, stop_hbm, values_hbm, table_hbm, out_ref,
    ids_ref, start_ref, stop_ref, values_ref, table_ref, sems,
):
    pairs = [
        (values_hbm, values_ref),
        (table_hbm, table_ref),
        (ids_hbm, ids_ref),
        (start_hbm, start_ref),
        (stop_hbm, stop_ref),
    ]
    copies = [
        pltpu.make_async_copy(source, target, sems.at[i])
        for i, (source, target) in enumerate(pairs)
    ]
    for copy in copies:
        copy.start()
    copies[3].wait()
    copies[4].wait()
    start, stop = cells_of(start_ref[...], stop_ref[...])
    for copy in copies[0:3]:
        copy.wait()
    chosen = lines_of(ids_ref[...])
    out_ref[:, 0, :] = x_body(
        start, stop, chosen, values_ref[...], table_ref[...], lane_roll
    )


def swap_blocks(tiles, roll):
    lane = lax.broadcasted_iota(jnp.int32, tiles[0].shape, 1)
    low64 = lane < 64
    even32 = (lane // 32) % 2 == 0
    q0, q1, q2, q3 = tiles
    q0, q2 = jnp.where(low64, q0, roll(q2, 64)), jnp.where(low64, roll(q0, 64), q2)
    q1, q3 = jnp.where(low64, q1, roll(q3, 64)), jnp.where(low64, roll(q1, 64), q3)
    q0, q1 = jnp.where(even32, q0, roll(q1, 32)), jnp.where(even32, roll(q0, 96), q1)
    q2, q3 = jnp.where(even32, q2, roll(q3, 32)), jnp.where(even32, roll(q2, 96), q3)
    return q0, q1, q2, q3


def lane_roll(values, shift):
    return pltpu.roll(values, shift, 1)


def z_body(arrived, table_ref, twiddle_ref, store, roll):
    rest = LINES_HERE - 256
    last = jnp.concatenate([arrived[:, 512:576], jnp.zeros((KXW, 64), F32)], axis=1)
    real = [arrived[:, 0:128], arrived[:, 128:256], last]
    imag = [arrived[:, 256:384], arrived[:, 384:512], roll(last, 128 - rest)]
    rows = [jnp.concatenate(pair, axis=0).T for pair in zip(real, imag)]
    rows = jnp.concatenate([rows[0], rows[1], rows[2][0:rest]], axis=0)
    spectrum = waves(rows, table_ref)
    for j, (re, im) in enumerate(twisted(spectrum, YD, twiddle_ref)):
        tiles = swap_blocks((re[0:24], re[24:48], im[0:24], im[24:48]), roll)
        for a in range(4):
            piece = 4 * j + a
            store(GY_ORDER.index(piece // 3), piece % 3, tiles[a])


def z_kernel(in_ref, table_ref, twiddle_ref, out_ref):
    def store(block, third, tile):
        out_ref[block, third * 24 : third * 24 + 24, :] = tile

    z_body(in_ref[:, 0, :], table_ref, twiddle_ref, store, lane_roll)


def y_waves(load, third, table_ref, roll):
    pieces = {}
    for e in range(3):
        rows = jnp.concatenate(
            [load(GY_ORDER.index(g), third * 24 + e * 8) for g in range(GY)], axis=0
        )
        flipped = jnp.concatenate([rows, roll(rows, 64)], axis=0).T
        pieces[e] = flipped[0:32]
        pieces[3 + e] = flipped[32:64]
    return waves(jnp.concatenate([pieces[u] for u in range(6)], axis=0), table_ref)


def y_kernel(
    in_ref, real_ref, imag_ref, table_ref, twiddle_ref, out_re_hbm, out_im_hbm,
    out_re_ref, out_im_ref, sems,
):
    def load(g, row):
        return in_ref[g, row : row + 8, :]

    copies = []
    spectrum = y_waves(load, 0, table_ref, lane_roll)
    for third in range(3):
        rows = slice(32 * third, 32 * third + 32)
        here = spectrum
        if third < 2:
            spectrum = y_waves(load, third + 1, table_ref, lane_roll)
        for j, (re, im) in enumerate(twisted(here, 32, twiddle_ref)):
            lanes = slice(WAVES * j, WAVES * (j + 1))
            s_re, s_im = real_ref[0, rows, lanes], imag_ref[0, rows, lanes]
            out_re_ref[0, rows, lanes] = s_re * re - s_im * im
            out_im_ref[0, rows, lanes] = s_re * im + s_im * re
        for i, (source, target) in enumerate(((out_re_ref, out_re_hbm), (out_im_ref, out_im_hbm))):
            copies.append(
                pltpu.make_async_copy(
                    source.at[:, rows, :], target.at[:, rows, :], sems.at[2 * third + i]
                )
            )
            copies[-1].start()
    for copy in copies:
        copy.wait()


PARAMS = pltpu.CompilerParams(vmem_limit_bytes=24 * 1024 * 1024)


def exchange(sent, axis, order):
    return lax.all_to_all(
        sent, axis, split_axis=0, concat_axis=0, tiled=True, axis_index_groups=[order]
    )


def in_hbm(array):
    return pltpu.with_memory_space_constraint(array, pltpu.HBM)


def on_device(line_values, line_ids, line_start, line_stop, spectrum_real, spectrum_imag):
    z_table = jnp.asarray(wave_tables(KX_ORDER))
    y_table = jnp.asarray(wave_tables(range(64), float(NG) ** (-1.5)))
    twiddle = jnp.asarray(twiddles())
    hbm = pl.BlockSpec(memory_space=pltpu.HBM)
    vmem = pl.BlockSpec(memory_space=pltpu.VMEM)
    sent = pl.pallas_call(
        x_kernel,
        out_shape=jax.ShapeDtypeStruct((KXW, 1, 2 * LINES_HERE), F32),
        in_specs=[hbm] * 5,
        out_specs=vmem,
        scratch_shapes=[
            pltpu.VMEM((1, LCAP), jnp.int32),
            pltpu.VMEM((1, LCAP), jnp.int32),
            pltpu.VMEM((1, LCAP), jnp.int32),
            pltpu.VMEM((LCAP, 2 * NG), F32),
            pltpu.VMEM((NG, 4 * KXW), BF16),
            pltpu.SemaphoreType.DMA((5,)),
        ],
        compiler_params=PARAMS,
        name="x_lines",
    )(
        in_hbm(line_ids.reshape(1, LCAP)),
        in_hbm(line_start.reshape(1, LCAP)),
        in_hbm(line_stop.reshape(1, LCAP)),
        in_hbm(line_values),
        in_hbm(jnp.asarray(x_tables())),
    )
    arrived = exchange(sent, "kx", KX_ORDER)
    sent = pl.pallas_call(
        z_kernel,
        out_shape=jax.ShapeDtypeStruct((GY, 72, 128), F32),
        compiler_params=PARAMS,
        name="z_rows",
    )(arrived, z_table, twiddle)
    arrived = exchange(sent, "gy", GY_ORDER)
    out = jax.ShapeDtypeStruct(spectrum_real.shape, F32)
    return pl.pallas_call(
        y_kernel,
        out_shape=(out, out),
        in_specs=[vmem] * 5,
        out_specs=(hbm, hbm),
        scratch_shapes=[
            pltpu.VMEM(spectrum_real.shape, F32),
            pltpu.VMEM(spectrum_real.shape, F32),
            pltpu.SemaphoreType.DMA((6,)),
        ],
        compiler_params=PARAMS,
        name="y_rows",
    )(arrived, spectrum_real, spectrum_imag, y_table, twiddle)


def solution(mesh):
    in_specs = (
        P(("kx", "gy"), None),
        P(("kx", "gy")),
        P(("kx", "gy")),
        P(("kx", "gy")),
        P("kx", "gy", None),
        P("kx", "gy", None),
    )
    out_specs = (P("kx", "gy", None), P("kx", "gy", None))
    return jax.shard_map(
        on_device, mesh=mesh, in_specs=in_specs, out_specs=out_specs, check_vma=False
    )
```
